32 devices in a mesh: pair: 8 (over z, x), tm: 4 (over y, core).
Axes of the slice: x: 2, y: 2, z: 4, core: 2. Of those that a mesh axis runs over, the one named last changes fastest.
Arguments:
- history: float32 [8192, 4096], P('tm', 'pair'), may hold values from -6 to 6
- round_index: int32 [1], replicated, may hold values from 0 to 14
Outputs:
- rotated: float32 [8192, 4096], P('tm', 'pair')
The draws below stay inside these ranges and needn't reach their ends.
Inputs may be any that keep to these rules, and one draw needn't show every extreme that they name: `round_index`: the same value on every device.
All inputs are finite; a program needn't handle non-finite values.
Results may differ from the reference program's by a relative error of at most 0.0003.
Values sent between devices are 32-bit elements; how exact they have to be, the bound alone decides.
No kernel may reach another device: no remote copies, remote signals or barrier semaphores. Data moves between devices by JAX's collectives and lax.ppermute only.
A program may use at most 64 MiB of HBM per device.

```python
import jax
import jax.numpy as jnp
from jax import lax

COLS = 256
STEPS = 4
SAMPLES = 8192
TAGS = 4096
N_PAIR = 8


def levels(own_key, shape, cuts, smallest, high):
    gain = 1.0
    for axis_at, parts in cuts:
        draws = jax.random.uniform(jax.random.fold_in(jax.random.fold_in(own_key, 6), axis_at), (parts,), jnp.float32, smallest / len(cuts), high / len(cuts))
        gain = gain * jnp.repeat(jnp.exp(draws), shape[axis_at] // parts).reshape((-1,) + (1,) * (len(shape) - 1 - axis_at))
    return gain


def normal_values(rng, extent, scale, most, cuts=(), held_as=jnp.bfloat16):
    factor_of = levels(rng, extent, cuts, -0.22, 0.18) if cuts else 1.0
    entries = jax.random.normal(rng, extent, jnp.float32) * scale * factor_of
    return jnp.minimum(jnp.maximum(entries, -most), most).astype(held_as)


def setup_inputs(seed: int = 0) -> dict:
    key_of = jax.random.split(jax.random.key(seed), 3)
    return {
        "history": normal_values(key_of[0], (SAMPLES, TAGS), 1.0, 6.0, ((0, 4), (1, 8)), jnp.float32),
        "round_index": jax.random.randint(key_of[1], (1,), 0, 2 * N_PAIR - 1).astype(jnp.int32),
    }


epsilon = 1e-06

def block_ids(round_index, pair_count):
    position = jnp.arange(pair_count, dtype=jnp.int32)
    cycle_len = 2 * pair_count - 1
    round_now = round_index[0].astype(jnp.int32)
    top_ids = jnp.where(position == 0, 0, 1 + jnp.mod(position - 1 - round_now, cycle_len)).astype(jnp.int32)
    bottom_ids = (1 + jnp.mod(2 * pair_count - 2 - position - round_now, cycle_len)).astype(jnp.int32)
    return (top_ids, bottom_ids)

def orientation(top_id, bottom_id, width):
    column = jnp.arange(2 * width, dtype=jnp.int32)
    global_id = jnp.where(column < width, top_id * width + column, bottom_id * width + column - width)
    return jnp.sign(global_id[None, :] - global_id[:, None]).astype(jnp.float32)

def start_iterate(gram_full, orient):
    diag_sq = jnp.diagonal(gram_full)
    skew_part = orient * gram_full / (diag_sq[:, None] + diag_sq[None, :] + epsilon)
    scale_norm = jnp.sqrt(1.0 + jnp.sum(skew_part * skew_part))
    identity = jnp.eye(gram_full.shape[0], dtype=jnp.float32)
    return (identity + skew_part) / scale_norm

def polar_step(factor):
    identity = jnp.eye(factor.shape[1], dtype=jnp.float32)
    square = jnp.dot(factor.T, factor, precision=lax.Precision.HIGHEST, preferred_element_type=jnp.float32)
    return jnp.dot(factor, 1.5 * identity - 0.5 * square, precision=lax.Precision.HIGHEST, preferred_element_type=jnp.float32)

def reference(history, round_index):
    pair_count = N_PAIR
    width = COLS
    blocks = history.reshape(SAMPLES, pair_count, 2 * width).transpose(1, 0, 2)
    top_ids, bottom_ids = block_ids(round_index, pair_count)

    def rotate_pair(inputs):
        columns, top_id, bottom_id = inputs
        gram_full = jnp.dot(columns.T, columns, precision=lax.Precision.HIGHEST, preferred_element_type=jnp.float32)
        factor = start_iterate(gram_full, orientation(top_id, bottom_id, width))
        for step in range(STEPS):
            factor = polar_step(factor)
        return jnp.dot(columns, factor, precision=lax.Precision.HIGHEST, preferred_element_type=jnp.float32)
    rotated = lax.map(rotate_pair, (blocks, top_ids, bottom_ids))
    top_out = rotated[:, :, :width]
    bottom_out = rotated[:, :, width:]
    new_top = jnp.concatenate([top_out[:1], bottom_out[:1], top_out[1:-1]], axis=0)
    new_bottom = jnp.concatenate([bottom_out[1:], top_out[-1:]], axis=0)
    joined = jnp.concatenate([new_top, new_bottom], axis=2)
    return joined.transpose(1, 0, 2).reshape(SAMPLES, TAGS)
```

```python
import jax
import jax.numpy as jnp
from jax import lax
from jax.experimental import pallas as pl
from jax.experimental.pallas import tpu as pltpu
from jax.sharding import PartitionSpec as P

STEPS = 4
TILE = 128
F32, BF16 = jnp.float32, jnp.bfloat16

epsilon = 1e-06

PLAN = ((4, 0), (4, 0), (8, 4))

VMEM_BYTES = 48 << 20
IN_VMEM = pl.BlockSpec(memory_space=pltpu.VMEM)
IN_SMEM = pl.BlockSpec(memory_space=pltpu.SMEM)
ANYWHERE = pl.BlockSpec(memory_space=pl.ANY)


def split(x):
    high = x.astype(BF16)
    return high, (x - high.astype(F32)).astype(BF16)


def product(a, b):
    return jnp.dot(a, b, preferred_element_type=F32)


def inner(a, b):
    return lax.dot_general(a, b, (((0,), (0,)), ((), ())), preferred_element_type=F32)


def params(**more):
    return pltpu.CompilerParams(vmem_limit_bytes=VMEM_BYTES, **more)


def upper_tiles(width):
    n = width // TILE
    at = [slice(i * TILE, (i + 1) * TILE) for i in range(n)]
    return list(enumerate((at[i], at[j]) for i in range(n) for j in range(i, n)))


def gram_kernel(core_ref, b_ref, out_ref, high_ref, cross_ref):
    high, low = split(b_ref[...])
    high_ref[...] = inner(high, high)
    cross_ref[...] = inner(high, low)
    core = core_ref[0]
    tiles = upper_tiles(b_ref.shape[1])
    half = len(tiles) // 2
    for k, (i, j) in tiles:
        at = slice(k % half * TILE, (k % half + 1) * TILE)
        out_ref[core ^ (k // half), at, :] = high_ref[i, j] + cross_ref[i, j] + cross_ref[j, i].T


def gram(core, b):
    rows, width = b.shape
    packed = len(upper_tiles(width)) // 2 * TILE
    return pl.pallas_call(
        gram_kernel,
        in_specs=[IN_SMEM, IN_VMEM],
        out_specs=IN_VMEM,
        out_shape=jax.ShapeDtypeStruct((2, packed, TILE), F32),
        scratch_shapes=[pltpu.VMEM((width, width), F32)] * 2,
        compiler_params=params(),
        cost_estimate=pl.CostEstimate(flops=0, bytes_accessed=0, transcendentals=0),
        name="gram",
    )(core, b)


def polar_kernel(at_ref, mine_ref, other_ref, _, high_ref, low_ref, x_ref, one_ref, two_ref):
    width = x_ref.shape[0]
    half = width // 2
    core, top_id, bottom_id, swapped = (at_ref[i] for i in range(4))
    tiles = upper_tiles(width)
    for k, (i, j) in tiles:
        per = len(tiles) // 2
        at = slice(k % per * TILE, (k % per + 1) * TILE)
        tile = jnp.where(core == k // per, mine_ref[at], other_ref[at])
        one_ref[i, j] = tile
        if i != j:
            one_ref[j, i] = tile.T
    row = lax.broadcasted_iota(jnp.int32, (width, width), 0)
    column = lax.broadcasted_iota(jnp.int32, (width, width), 1)
    on_diagonal = row == column

    def global_id(c):
        return jnp.where(c < half, top_id * half + c, bottom_id * half + c - half)

    row_id = global_id(lax.broadcasted_iota(jnp.int32, (width, 1), 0))
    column_id = global_id(lax.broadcasted_iota(jnp.int32, (1, width), 1))
    gram_full = one_ref[...]
    diagonal = jnp.where(on_diagonal, gram_full, 0.0)
    across = jnp.sum(diagonal, axis=0, keepdims=True)
    down = jnp.sum(diagonal, axis=1, keepdims=True)
    skew = gram_full / (down + across + epsilon)
    skew = jnp.where(column_id > row_id, skew, jnp.where(column_id < row_id, -skew, 0.0))
    norm = jnp.sqrt(1.0 + jnp.sum(skew * skew))
    x_ref[...] = (jnp.where(on_diagonal, 1.0, 0.0) + skew) / norm
    for _ in range(STEPS):
        high, low = split(x_ref[...])
        one_ref[...] = inner(high, high)
        two_ref[...] = inner(high, low)
        square = one_ref[...] + two_ref[...] + two_ref[...].T
        turn_high, turn_low = split(jnp.where(on_diagonal, 1.5, 0.0) - 0.5 * square)
        x_ref[...] = product(high, turn_high)
        one_ref[...] = product(high, turn_low)
        two_ref[...] = product(low, turn_high)
        x_ref[...] = x_ref[...] + (one_ref[...] + two_ref[...])
    for flag, (first, second) in enumerate((((0, half), (half, width)), ((half, width), (0, half)))):

        @pl.when(swapped == flag)
        def _():
            for to, (begin, end) in ((0, first), (half, second)):
                high, low = split(x_ref[:, begin:end])
                high_ref[:, to : to + half] = high
                low_ref[:, to : to + half] = low


def polar(at, mine, other, after, width):
    return pl.pallas_call(
        polar_kernel,
        in_specs=[IN_SMEM, IN_VMEM, IN_VMEM, ANYWHERE],
        out_specs=[IN_VMEM, IN_VMEM],
        out_shape=[jax.ShapeDtypeStruct((width, width), BF16)] * 2,
        scratch_shapes=[pltpu.VMEM((width, width), F32)] * 3,
        compiler_params=params(),
        cost_estimate=pl.CostEstimate(flops=0, bytes_accessed=0, transcendentals=0),
        name="polar",
    )(at, mine, other, after)


def turn_kernel(start, b_ref, high_ref, low_ref, first_ref, second_ref, rows_ref, sem):
    load = pltpu.make_async_copy(b_ref.at[pl.ds(start, rows_ref.shape[0])], rows_ref, sem)
    load.start()
    load.wait()
    high, low = split(rows_ref[...])
    half = first_ref.shape[1]
    for out_ref, at in ((first_ref, slice(0, half)), (second_ref, slice(half, 2 * half))):
        w_high, w_low = high_ref[:, at], low_ref[:, at]
        out_ref[...] = product(high, w_high) + product(high, w_low) + product(low, w_high)


def turn(b, start, count, w):
    width = b.shape[1]

    def kernel(*refs):
        turn_kernel(start, *refs)

    return pl.pallas_call(
        kernel,
        in_specs=[ANYWHERE, IN_VMEM, IN_VMEM],
        out_specs=[IN_VMEM, IN_VMEM],
        out_shape=[jax.ShapeDtypeStruct((count, width // 2), F32)] * 2,
        scratch_shapes=[pltpu.VMEM((count, width), F32), pltpu.SemaphoreType.DMA],
        compiler_params=params(),
        cost_estimate=pl.CostEstimate(flops=0, bytes_accessed=0, transcendentals=0),
        name="turn",
    )(b, *w)


def take(b, start, count, after):
    width = b.shape[1]

    def kernel(b_ref, _, out_ref, sem):
        copy = pltpu.make_async_copy(b_ref.at[pl.ds(start, count)], out_ref, sem)
        copy.start()
        copy.wait()

    return pl.pallas_call(
        kernel,
        in_specs=[ANYWHERE, ANYWHERE],
        out_specs=IN_VMEM,
        out_shape=jax.ShapeDtypeStruct((count, width), F32),
        scratch_shapes=[pltpu.SemaphoreType.DMA],
        compiler_params=params(),
        cost_estimate=pl.CostEstimate(flops=0, bytes_accessed=0, transcendentals=0),
        name="take",
    )(b, after)


def own_kernel(start, end_ref, b_ref, high_ref, low_ref, out_ref, rows_ref, sem):
    half = out_ref.shape[1]
    for which, at in ((1, slice(half, 2 * half)), (2, slice(0, half))):

        @pl.when(end_ref[0] == which)
        def _():
            load = pltpu.make_async_copy(b_ref.at[pl.ds(start, rows_ref.shape[0])], rows_ref, sem)
            load.start()
            load.wait()
            high, low = split(rows_ref[...])
            w_high, w_low = high_ref[:, at], low_ref[:, at]
            out_ref[...] = product(high, w_high) + product(high, w_low) + product(low, w_high)


def own(end, b, start, count, w):
    width = b.shape[1]

    def kernel(*refs):
        own_kernel(start, *refs)

    return pl.pallas_call(
        kernel,
        in_specs=[IN_SMEM, ANYWHERE, IN_VMEM, IN_VMEM],
        out_specs=IN_VMEM,
        out_shape=jax.ShapeDtypeStruct((count, width // 2), F32),
        scratch_shapes=[pltpu.VMEM((count, width), F32), pltpu.SemaphoreType.DMA],
        compiler_params=params(),
        cost_estimate=pl.CostEstimate(flops=0, bytes_accessed=0, transcendentals=0),
        name="own",
    )(end, b, *w)


def join_kernel(places, choice_ref, *refs):
    out_ref, held_ref, load_sem, store_sem = refs[-4:]
    half = out_ref.shape[1] // 2
    loads, stores = [], []
    taken = 0
    for k, (start, count, sources) in enumerate(places):
        for side in (0, 1):
            n = sources[side]
            for s in range(n):
                into = held_ref.at[pl.ds(start, count), pl.ds(side * half, half)]
                copy = pltpu.make_async_copy(refs[taken + s], into, load_sem.at[2 * k + side])

                @pl.when(choice_ref[2 * k + side] == s)
                def _():
                    copy.start()

            loads.append(copy)
            taken += n
    for k, (start, count, _) in enumerate(places):
        loads[2 * k].wait()
        loads[2 * k + 1].wait()
        at = pl.ds(start, count)
        stores.append(pltpu.make_async_copy(held_ref.at[at], out_ref.at[at], store_sem.at[k]))
        stores[-1].start()
    for copy in stores:
        copy.wait()


def join(choice, chunks, rows, width):
    places = [(start, count, (len(left), len(right))) for start, count, left, right in chunks]
    arrays = [a for _, _, left, right in chunks for a in (*left, *right)]

    def kernel(*refs):
        join_kernel(places, *refs)

    return pl.pallas_call(
        kernel,
        in_specs=[IN_SMEM] + [ANYWHERE] * len(arrays),
        out_specs=ANYWHERE,
        out_shape=jax.ShapeDtypeStruct((rows, width), F32),
        scratch_shapes=[
            pltpu.VMEM((rows, width), F32),
            pltpu.SemaphoreType.DMA((2 * len(chunks),)),
            pltpu.SemaphoreType.DMA((len(chunks),)),
        ],
        compiler_params=params(),
        cost_estimate=pl.CostEstimate(flops=0, bytes_accessed=0, transcendentals=0),
        name="join",
    )(choice, *arrays)


def shards(history, round_index):
    rows, width = history.shape
    pairs = lax.axis_size("pair")
    levels = pairs // 2
    position = lax.axis_index("pair")
    partner = position ^ 1
    even = position % 2 == 0
    first, last = position == 0, position == pairs - 1
    core, row_half = lax.axis_index("tm") % 2, lax.axis_index("tm") // 2
    cycle_len = 2 * pairs - 1
    round_now = round_index[0]
    swap_pairs = [(p, p ^ 1) for p in range(pairs)]
    swap_cores = [(i, i ^ 1) for i in range(4)]
    swap_rows = [(i, i ^ 2) for i in range(4)]

    def ids(p):
        top_id = jnp.where(p == 0, 0, 1 + jnp.mod(p - 1 - round_now, cycle_len))
        bottom_id = 1 + jnp.mod(2 * pairs - 2 - p - round_now, cycle_len)
        return top_id, bottom_id

    def is_early(p, threshold):
        level = p // 2
        return (p % 2 == 0) & (level >= threshold) | (p % 2 == 1) & (level <= levels - 1 - threshold)

    chunks = []
    begin = 0
    for sixteenths, quarter in PLAN:
        count = rows * sixteenths // 16
        chunks.append((begin, count, quarter * levels // 4))
        begin += count

    def swap_early(k, after):
        begin, count, threshold = chunks[k]
        sent = [(p, p ^ 1) for p in range(pairs) if is_early(p, threshold)]
        return lax.ppermute(take(history, begin, count, after), "pair", sent)

    early = [k for k, chunk in enumerate(chunks) if chunk[2] < levels]
    from_partner = {0: swap_early(0, round_index)}

    packed = gram(jnp.stack([core]), history)
    summed = packed[0] + lax.ppermute(packed[1], "tm", swap_cores)
    mine = summed + lax.ppermute(summed, "tm", swap_rows)
    other = lax.ppermute(mine, "tm", swap_cores)

    piece = mine.shape[0] // 2
    part = lax.ppermute(lax.dynamic_slice_in_dim(mine, row_half * piece, piece), "pair", swap_pairs)
    for k in early[1:]:
        from_partner[k] = swap_early(k, other)
    part_2 = lax.ppermute(part, "tm", swap_rows)
    mine_q = jnp.where(row_half == 0, jnp.concatenate([part, part_2]), jnp.concatenate([part_2, part]))
    other_q = lax.ppermute(mine_q, "tm", swap_cores)

    flag = first.astype(jnp.int32)
    w = polar(jnp.stack([core, *ids(position), flag]), mine, other, from_partner[0], width)

    late = {}
    for k, (begin, count, threshold) in enumerate(chunks):
        if threshold > 0:
            right, left = turn(history, begin, count, w)
            to_right = [(p, p + 1) for p in range(pairs - 1) if not is_early(p, threshold)]
            to_left = [(p, p - 1) for p in range(1, pairs) if not is_early(p, threshold)]
            late[k] = (right, left, lax.ppermute(right, "pair", to_right), lax.ppermute(left, "pair", to_left))

    flag_q = (even | (partner == 0)).astype(jnp.int32)
    w_q = polar(jnp.stack([core, *ids(partner), flag_q]), mine_q, other_q, from_partner[early[-1]], width)
    end = jnp.stack([first + 2 * last]).astype(jnp.int32)

    joined, choice = [], []
    for k, (begin, count, threshold) in enumerate(chunks):
        left_from, right_from = [], []
        top_choice, bottom_choice = 0, 0
        if threshold < levels:
            near, far = turn(from_partner[k], 0, count, w_q)
            onward = [(p ^ 1, p - 1) for p in range(2, pairs, 2) if is_early(p, threshold)]
            onward += [(p ^ 1, p + 1) for p in range(1, pairs - 1, 2) if is_early(p, threshold)]
            passed = lax.ppermute(far, "pair", onward)
            left_from += [near, passed]
            right_from += [near, passed]
            top_choice = jnp.where(even, 1, 0)
            bottom_choice = jnp.where(even, 0, 1)
            if threshold == 0:
                alone = own(end, history, begin, count, w)
                left_from.append(alone)
                right_from.append(alone)
                top_choice = jnp.where(first, 2, top_choice)
                bottom_choice = jnp.where(last, 2, bottom_choice)
        if threshold > 0:
            n = len(left_from)
            right, left, from_left, from_right = late[k]
            left_from += [from_left, left]
            right_from += [from_right, right]
            top_choice = jnp.where(is_early(position - 1, threshold) & ~first, top_choice, n)
            bottom_choice = jnp.where(is_early(position + 1, threshold) & ~last, bottom_choice, n)
            top_choice = jnp.where(first, n + 1, top_choice)
            bottom_choice = jnp.where(last, n + 1, bottom_choice)
        joined.append((begin, count, left_from, right_from))
        choice += [top_choice, bottom_choice]
    return join(jnp.stack(choice).astype(jnp.int32), joined, rows, width)


def solution(mesh):
    in_specs = (P("tm", "pair"), P())
    out_specs = P("tm", "pair")
    return jax.shard_map(shards, mesh=mesh, in_specs=in_specs, out_specs=out_specs, check_vma=False)
```

```python
import jax
import jax.numpy as jnp
from jax import lax
from jax.experimental import pallas as pl
from jax.experimental.pallas import tpu as pltpu
from jax.sharding import PartitionSpec as P

STEPS = 4
TILE = 128
F32, BF16 = jnp.float32, jnp.bfloat16

epsilon = 1e-06

PLAN = ((0, (6, 9)), (0, (13,)), (4, (36,)))

MIB = 1 << 20
LONG = 10**12
WHOLE = pl.BlockSpec()
IN_VMEM = pl.BlockSpec(memory_space=pltpu.VMEM)
IN_SMEM = pl.BlockSpec(memory_space=pltpu.SMEM)
ANYWHERE = pl.BlockSpec(memory_space=pl.ANY)


def call(kernel, name, operands, in_specs, outs, out_specs, scratch=(), after=(), vmem=56, flops=0, **more):
    given, late = len(operands), len(after)

    def body(*refs):
        kernel(*refs[:given], *refs[given + late :])

    return pl.pallas_call(
        body,
        in_specs=[*in_specs, *[ANYWHERE] * late],
        out_specs=out_specs,
        out_shape=outs,
        scratch_shapes=scratch,
        compiler_params=pltpu.CompilerParams(vmem_limit_bytes=vmem * MIB),
        cost_estimate=pl.CostEstimate(flops=flops, bytes_accessed=0, transcendentals=0),
        name=name,
        **more,
    )(*operands, *after)


def shape(*dims, dtype=F32):
    return jax.ShapeDtypeStruct(dims, dtype)


def split(x):
    high = x.astype(BF16)
    return high, (x - high.astype(F32)).astype(BF16)


def product(a, b):
    return jnp.dot(a, b, preferred_element_type=F32)


def inner(a, b):
    return lax.dot_general(a, b, (((0,), (0,)), ((), ())), preferred_element_type=F32)


def upper_tiles(width):
    n = width // TILE
    at = [slice(i * TILE, (i + 1) * TILE) for i in range(n)]
    return list(enumerate((at[i], at[j]) for i in range(n) for j in range(i, n)))


def gram(core, b, pieces, after, parts=4):
    rows, width = b.shape
    tiles = upper_tiles(width)
    half = len(tiles) // 2

    def kernel(core_ref, b_ref, *refs):
        mine_ref, other_ref, *copies = refs[:-5]
        rows_ref, high_ref, cross_ref, load_sem, store_sem = refs[-5:]
        loads = [
            pltpu.make_async_copy(b_ref.at[pl.ds(p * (rows // parts), rows // parts)], at, load_sem.at[p])
            for p, at in enumerate(rows_ref.at[pl.ds(p * (rows // parts), rows // parts)] for p in range(parts))
        ]
        stores = [
            pltpu.make_async_copy(rows_ref.at[pl.ds(*piece)], copies[k], store_sem.at[k])
            for k, piece in enumerate(pieces)
        ]
        for load in loads:
            load.start()
        for p, load in enumerate(loads):
            load.wait()
            high, low = split(rows_ref[p * (rows // parts) : (p + 1) * (rows // parts)])
            high_ref[p] = inner(high, high)
            cross_ref[p] = inner(high, low)
        for store in stores:
            store.start()

        for flag, outs in enumerate(((mine_ref, other_ref), (other_ref, mine_ref))):

            @pl.when(core_ref[0] == flag)
            def _():
                for k, (i, j) in tiles:
                    tile = sum(high_ref[p, i, j] + cross_ref[p, i, j] for p in range(parts))
                    at = slice(k % half * TILE, (k % half + 1) * TILE)
                    outs[k // half][at, :] = tile + sum(cross_ref[p, j, i] for p in range(parts)).T

        for store in stores:
            store.wait()

    outs = [shape(half * TILE, TILE)] * 2 + [shape(count, width) for _, count in pieces]
    scratch = [
        pltpu.VMEM((rows, width), F32),
        *[pltpu.VMEM((parts, width, width), F32)] * 2,
        pltpu.SemaphoreType.DMA((parts,)),
        pltpu.SemaphoreType.DMA((max(1, len(pieces)),)),
    ]
    specs = [IN_VMEM] * 2 + [ANYWHERE] * len(pieces)
    return call(kernel, "gram", (core, b), [IN_SMEM, ANYWHERE], outs, specs, scratch, after, flops=LONG)


def add(a, b, after):
    def kernel(a_ref, b_ref, out_ref):
        out_ref[...] = a_ref[...] + b_ref[...]

    return call(kernel, "add", (a, b), [IN_VMEM] * 2, shape(*a.shape), IN_VMEM, after=after, vmem=8)


def add_and_cut(second, a, b, after):
    n = a.shape[0] // 2

    def kernel(second_ref, a_ref, b_ref, out_ref, part_ref):
        out_ref[...] = a_ref[...] + b_ref[...]
        for flag, at in ((0, slice(0, n)), (1, slice(n, 2 * n))):

            @pl.when(second_ref[0] == flag)
            def _():
                part_ref[...] = a_ref[at, :] + b_ref[at, :]

    outs = [shape(*a.shape), shape(n, a.shape[1])]
    specs = [IN_SMEM, IN_VMEM, IN_VMEM]
    return call(kernel, "add", (second, a, b), specs, outs, [IN_VMEM] * 2, after=after, vmem=8)


def merge_kernel(second_ref, a_ref, b_ref, out_ref):
    n = a_ref.shape[0]
    for flag, (x_ref, y_ref) in enumerate(((a_ref, b_ref), (b_ref, a_ref))):

        @pl.when(second_ref[0] == flag)
        def _():
            out_ref[:n] = x_ref[...]
            out_ref[n:] = y_ref[...]


def merge(second, a, b, after):
    out = shape(2 * a.shape[0], a.shape[1])
    return call(merge_kernel, "merge", (second, a, b), [IN_SMEM, IN_VMEM, IN_VMEM], out, IN_VMEM, after=after, vmem=8)


def polar_kernel(at_ref, mine_ref, other_ref, high_ref, low_ref, x_ref, one_ref, two_ref):
    width = x_ref.shape[0]
    half = width // 2
    core, top_id, bottom_id, swapped = (at_ref[i] for i in range(4))
    tiles = upper_tiles(width)
    for k, (i, j) in tiles:
        per = len(tiles) // 2
        at = slice(k % per * TILE, (k % per + 1) * TILE)
        tile = jnp.where(core == k // per, mine_ref[at], other_ref[at])
        one_ref[i, j] = tile
        if i != j:
            one_ref[j, i] = tile.T
    row = lax.broadcasted_iota(jnp.int32, (width, width), 0)
    column = lax.broadcasted_iota(jnp.int32, (width, width), 1)
    on_diagonal = row == column

    def global_id(c):
        return jnp.where(c < half, top_id * half + c, bottom_id * half + c - half)

    row_id = global_id(lax.broadcasted_iota(jnp.int32, (width, 1), 0))
    column_id = global_id(lax.broadcasted_iota(jnp.int32, (1, width), 1))
    gram_full = one_ref[...]
    diagonal = jnp.where(on_diagonal, gram_full, 0.0)
    across = jnp.sum(diagonal, axis=0, keepdims=True)
    down = jnp.sum(diagonal, axis=1, keepdims=True)
    skew = gram_full / (down + across + epsilon)
    skew = jnp.where(column_id > row_id, skew, jnp.where(column_id < row_id, -skew, 0.0))
    norm = jnp.sqrt(1.0 + jnp.sum(skew * skew))
    x_ref[...] = (jnp.where(on_diagonal, 1.0, 0.0) + skew) / norm
    for _ in range(STEPS):
        high, low = split(x_ref[...])
        one_ref[...] = inner(high, high)
        two_ref[...] = inner(high, low)
        square = one_ref[...] + two_ref[...] + two_ref[...].T
        turn_high, turn_low = split(jnp.where(on_diagonal, 1.5, 0.0) - 0.5 * square)
        x_ref[...] = product(high, turn_high)
        one_ref[...] = product(high, turn_low)
        two_ref[...] = product(low, turn_high)
        x_ref[...] = x_ref[...] + (one_ref[...] + two_ref[...])
    for flag, (first, second) in enumerate((((0, half), (half, width)), ((half, width), (0, half)))):

        @pl.when(swapped == flag)
        def _():
            for to, (begin, end) in ((0, first), (half, second)):
                high, low = split(x_ref[:, begin:end])
                high_ref[:, to : to + half] = high
                low_ref[:, to : to + half] = low


def polar(at, mine, other, width, after=()):
    specs = [IN_SMEM, IN_VMEM, IN_VMEM]
    outs = [shape(width, width, dtype=BF16)] * 2
    scratch = [pltpu.VMEM((width, width), F32)] * 3
    return call(polar_kernel, "polar", (at, mine, other), specs, outs, [IN_VMEM] * 2, scratch, after, 24, LONG)


def times(rows, w_high, w_low):
    high, low = split(rows)
    return product(high, w_high) + product(high, w_low) + product(low, w_high)


def turn_kernel(b_ref, high_ref, low_ref, first_ref, second_ref):
    half = first_ref.shape[1]
    for out_ref, at in ((first_ref, slice(0, half)), (second_ref, slice(half, 2 * half))):
        out_ref[...] = times(b_ref[...], high_ref[:, at], low_ref[:, at])


def row_blocks(count):
    return next(count // n for n in range(1, count) if count % n == 0 and count // n <= 512 and count // n % 16 == 0)


def turn(b, start, count, w, after=()):
    width = b.shape[1]
    rows = row_blocks(count)
    part = pl.BlockSpec((pl.Element(rows), pl.Element(width)), lambda i: (pl.multiple_of(start + i * rows, 16), 0))
    whole = pl.BlockSpec((width, width), lambda i: (0, 0))
    out = pl.BlockSpec((rows, width // 2), lambda i: (i, 0))
    outs = [shape(count, width // 2)] * 2
    return call(turn_kernel, "turn", (b, *w), [part, whole, whole], outs, [out, out], after=after, vmem=24, grid=(count // rows,))


def turn_all(arrays, w, after=()):
    width = w[0].shape[0]
    half = width // 2

    def kernel(*refs):
        (high_ref, low_ref), parts, outs = refs[:2], refs[2:-2], refs[-2:]
        begin = 0
        for b_ref in parts:
            rows = pl.ds(begin, b_ref.shape[0])
            for out_ref, at in zip(outs, (slice(0, half), slice(half, width)), strict=True):
                out_ref[rows, :] = times(b_ref[...], high_ref[:, at], low_ref[:, at])
            begin += b_ref.shape[0]

    outs = [shape(sum(b.shape[0] for b in arrays), half)] * 2
    return call(kernel, "turn", (*w, *arrays), [WHOLE] * (2 + len(arrays)), outs, [WHOLE] * 2, after=after, vmem=24)


def take(b, pieces):
    n = len(pieces)

    def kernel(b_ref, *refs):
        copies = [
            pltpu.make_async_copy(b_ref.at[pl.ds(*piece)], refs[k], refs[n].at[k]) for k, piece in enumerate(pieces)
        ]
        for copy in copies:
            copy.start()
        for copy in copies:
            copy.wait()

    outs = [shape(count, b.shape[1]) for _, count in pieces]
    return call(kernel, "take", (b,), [ANYWHERE], outs, [IN_VMEM] * n, [pltpu.SemaphoreType.DMA((n,))])


def own(end, b, start, count, w, after=()):
    width = b.shape[1]
    half = width // 2

    def kernel(end_ref, b_ref, high_ref, low_ref, out_ref, rows_ref, sem):
        for which, at in ((1, slice(half, width)), (2, slice(0, half))):

            @pl.when(end_ref[0] == which)
            def _():
                load = pltpu.make_async_copy(b_ref.at[pl.ds(start, count)], rows_ref, sem)
                load.start()
                load.wait()
                out_ref[...] = times(rows_ref[...], high_ref[:, at], low_ref[:, at])

    specs = [IN_SMEM, ANYWHERE, WHOLE, WHOLE]
    scratch = [pltpu.VMEM((count, width), F32), pltpu.SemaphoreType.DMA]
    return call(kernel, "own", (end, b, *w), specs, shape(count, half), WHOLE, scratch, after)


def join(choice, groups, rows, width, into=None):
    sources = [s if isinstance(s, tuple) else (s, 0) for _, _, left, right in groups for s in (*left, *right)]
    arrays = [array for array, _ in sources]
    half = width // 2
    lowest = min(group[0] for group in groups)
    held_rows = max(group[0] + group[1] for group in groups) - lowest

    def kernel(choice_ref, *refs):
        out_ref, held_ref, load_sem, store_sem = refs[-4:]
        loads, stores, taken = [], [], 0
        for k, (start, count, *sides) in enumerate(groups):
            for side, n in enumerate(len(one) for one in sides):
                place = held_ref.at[pl.ds(start - lowest, count), pl.ds(side * half, half)]
                for s in range(n):
                    rows_of_s = refs[taken + s].at[pl.ds(sources[taken + s][1], count)]
                    copy = pltpu.make_async_copy(rows_of_s, place, load_sem.at[2 * k + side])

                    @pl.when(choice_ref[2 * k + side] == s)
                    def _():
                        copy.start()

                loads.append(copy)
                taken += n
        for k, (start, count, *_) in enumerate(groups):
            loads[2 * k].wait()
            loads[2 * k + 1].wait()
            place = held_ref.at[pl.ds(start - lowest, count)]
            stores.append(pltpu.make_async_copy(place, out_ref.at[pl.ds(start, count)], store_sem.at[k]))
            stores[-1].start()
        for copy in stores:
            copy.wait()

    scratch = [
        pltpu.VMEM((held_rows, width), F32),
        pltpu.SemaphoreType.DMA((2 * len(groups),)),
        pltpu.SemaphoreType.DMA((len(groups),)),
    ]
    operands = (choice, *arrays)
    more = {}
    if into is not None:
        operands += (into,)
        more["input_output_aliases"] = {len(operands) - 1: 0}
    specs = [IN_SMEM] + [ANYWHERE] * (len(operands) - 1)
    return call(kernel, "join", operands, specs, shape(rows, width), ANYWHERE, scratch, vmem=8, **more)


def shards(history, round_index):
    rows, width = history.shape
    pairs = lax.axis_size("pair")
    levels = pairs // 2
    position = lax.axis_index("pair")
    partner = position ^ 1
    even = position % 2 == 0
    first, last = position == 0, position == pairs - 1
    core, row_half = lax.axis_index("tm") % 2, lax.axis_index("tm") // 2
    cycle_len = 2 * pairs - 1
    round_now = round_index[0]
    swap_pairs = [(p, p ^ 1) for p in range(pairs)]
    swap_cores = [(i, i ^ 1) for i in range(4)]
    swap_rows = [(i, i ^ 2) for i in range(4)]

    def ids(p):
        top_id = jnp.where(p == 0, 0, 1 + jnp.mod(p - 1 - round_now, cycle_len))
        bottom_id = 1 + jnp.mod(2 * pairs - 2 - p - round_now, cycle_len)
        return top_id, bottom_id

    def is_early(p, threshold):
        level = p // 2
        return (p % 2 == 0) & (level >= threshold) | (p % 2 == 1) & (level <= levels - 1 - threshold)

    groups, pieces = [], []
    begin = 0
    for quarter, parts in PLAN:
        counts = [rows * part // 64 for part in parts]
        groups.append((begin, sum(counts), quarter * levels // 4))
        pieces.append([(begin + sum(counts[:i]), count) for i, count in enumerate(counts)])
        begin += sum(counts)
    early = [k for k, group in enumerate(groups) if group[2] < levels]

    def sent_early(k, rows_of_k):
        return lax.ppermute(rows_of_k, "pair", [(p, p ^ 1) for p in range(pairs) if is_early(p, groups[k][2])])

    from_partner = {k: [] for k in early}
    taken = take(history, pieces[early[0]])
    from_partner[early[0]] = [sent_early(early[0], a) for a in taken]

    later = [(k, piece) for k in early[1:] for piece in pieces[k]]
    keep, give, *copies = gram(jnp.stack([core]), history, [piece for _, piece in later], taken)
    summed = add(keep, lax.ppermute(give, "tm", swap_cores), from_partner[early[0]][:1])
    from_row = lax.ppermute(summed, "tm", swap_rows)
    second = jnp.stack([row_half])
    mine, part = add_and_cut(second, summed, from_row, from_partner[early[0]][1:])
    other = lax.ppermute(mine, "tm", swap_cores)
    part = lax.ppermute(part, "pair", swap_pairs)
    for (k, _), a in zip(later, copies, strict=True):
        from_partner[k].append(sent_early(k, a))

    w = polar(jnp.stack([core, *ids(position), first.astype(jnp.int32)]), mine, other, width, (part,))
    late = {}
    for k, (begin, count, threshold) in enumerate(groups):
        if threshold > 0:
            right, left = turn(history, begin, count, w)
            to_right = [(p, p + 1) for p in range(pairs - 1) if not is_early(p, threshold)]
            to_left = [(p, p - 1) for p in range(1, pairs) if not is_early(p, threshold)]
            late[k] = (right, left, lax.ppermute(right, "pair", to_right), lax.ppermute(left, "pair", to_left))

    part_2 = lax.ppermute(part, "tm", swap_rows)
    mine_q = merge(second, part, part_2, [late[k][0] for k in late])
    other_q = lax.ppermute(mine_q, "tm", swap_cores)
    flag_q = (even | (partner == 0)).astype(jnp.int32)
    w_q = polar(jnp.stack([core, *ids(partner), flag_q]), mine_q, other_q, width, from_partner[early[1]])
    end = jnp.stack([first + 2 * last]).astype(jnp.int32)
    near, passed = {}, {}
    always = [k for k in early if groups[k][2] == 0]
    after = ()
    for k in early:
        threshold = groups[k][2]
        near[k], far = turn_all(from_partner[k], w_q, after)
        onward = [(p ^ 1, p - 1) for p in range(2, pairs, 2) if is_early(p, threshold)]
        onward += [(p ^ 1, p + 1) for p in range(1, pairs - 1, 2) if is_early(p, threshold)]
        passed[k] = lax.ppermute(far, "pair", onward)
        if k == early[0]:
            alone = own(end, history, groups[always[0]][0], sum(groups[k][1] for k in always), w, (far,))
            after = (alone, passed[k])

    ready, joined = {}, None
    for k, (begin, count, threshold) in enumerate(groups):
        left_from, right_from = [], []
        top_choice, bottom_choice = 0, 0
        if k in near:
            left_from += [near[k], passed[k]]
            right_from += [near[k], passed[k]]
            top_choice = jnp.where(even, 1, 0)
            bottom_choice = jnp.where(even, 0, 1)
        if k in always:
            left_from.append((alone, begin))
            right_from.append((alone, begin))
            top_choice = jnp.where(first, 2, top_choice)
            bottom_choice = jnp.where(last, 2, bottom_choice)
        if k in late:
            n = len(left_from)
            right, left, from_left, from_right = late[k]
            left_from += [from_left, left]
            right_from += [from_right, right]
            top_choice = jnp.where(is_early(position - 1, threshold) & ~first, top_choice, n)
            bottom_choice = jnp.where(is_early(position + 1, threshold) & ~last, bottom_choice, n)
            top_choice = jnp.where(first, n + 1, top_choice)
            bottom_choice = jnp.where(last, n + 1, bottom_choice)
        ready[k] = (begin, count, left_from, right_from), [top_choice, bottom_choice]
    for which in (early, [k for k in ready if k not in early]):
        choice = [c for k in which for c in ready[k][1]]
        joined = join(jnp.stack(choice).astype(jnp.int32), [ready[k][0] for k in which], rows, width, joined)
    return joined


def solution(mesh):
    in_specs = (P("tm", "pair"), P())
    out_specs = P("tm", "pair")
    return jax.shard_map(shards, mesh=mesh, in_specs=in_specs, out_specs=out_specs, check_vma=False)
```

```python
import jax
import jax.numpy as jnp
from jax import lax
from jax.experimental import pallas as pl
from jax.experimental.pallas import tpu as pltpu
from jax.sharding import PartitionSpec as P

STEPS = 4
TILE = 128
F32, BF16 = jnp.float32, jnp.bfloat16

epsilon = 1e-06

PLAN = ((0, (6, 12)), (0, (14,)), (4, (32,)))

MIB = 1 << 20
LONG = 10**12
WHOLE = pl.BlockSpec()
IN_VMEM = pl.BlockSpec(memory_space=pltpu.VMEM)
IN_SMEM = pl.BlockSpec(memory_space=pltpu.SMEM)
ANYWHERE = pl.BlockSpec(memory_space=pl.ANY)


def call(kernel, name, operands, in_specs, outs, out_specs, scratch=(), after=(), vmem=56, flops=0, **more):
    given, late = len(operands), len(after)

    def body(*refs):
        kernel(*refs[:given], *refs[given + late :])

    return pl.pallas_call(
        body,
        in_specs=[*in_specs, *[ANYWHERE] * late],
        out_specs=out_specs,
        out_shape=outs,
        scratch_shapes=scratch,
        compiler_params=pltpu.CompilerParams(vmem_limit_bytes=vmem * MIB),
        cost_estimate=pl.CostEstimate(flops=flops, bytes_accessed=0, transcendentals=0),
        name=name,
        **more,
    )(*operands, *after)


def shape(*dims, dtype=F32):
    return jax.ShapeDtypeStruct(dims, dtype)


def split(x):
    high = x.astype(BF16)
    return high, (x - high.astype(F32)).astype(BF16)


def product(a, b):
    return jnp.dot(a, b, preferred_element_type=F32)


def inner(a, b):
    return lax.dot_general(a, b, (((0,), (0,)), ((), ())), preferred_element_type=F32)


def upper_tiles(width):
    n = width // TILE
    at = [slice(i * TILE, (i + 1) * TILE) for i in range(n)]
    return list(enumerate((at[i], at[j]) for i in range(n) for j in range(i, n)))


def gram(core, b, pieces, kept, after, parts=4):
    rows, width = b.shape
    tiles = upper_tiles(width)
    half = len(tiles) // 2

    def kernel(core_ref, b_ref, *refs):
        mine_ref, other_ref, *copies = refs[:-5]
        rows_ref, high_ref, cross_ref, load_sem, store_sem = refs[-5:]
        loads = [
            pltpu.make_async_copy(b_ref.at[pl.ds(p * (rows // parts), rows // parts)], at, load_sem.at[p])
            for p, at in enumerate(rows_ref.at[pl.ds(p * (rows // parts), rows // parts)] for p in range(parts))
        ]
        stores = [
            pltpu.make_async_copy(rows_ref.at[pl.ds(*piece)], copies[k], store_sem.at[k])
            for k, piece in enumerate((*pieces, *kept))
        ]
        for load in loads:
            load.start()
        for p, load in enumerate(loads):
            load.wait()
            high, low = split(rows_ref[p * (rows // parts) : (p + 1) * (rows // parts)])
            high_ref[p] = inner(high, high)
            cross_ref[p] = inner(high, low)
        for store in stores:
            store.start()

        for flag, outs in enumerate(((mine_ref, other_ref), (other_ref, mine_ref))):

            @pl.when(core_ref[0] == flag)
            def _():
                for k, (i, j) in tiles:
                    tile = sum(high_ref[p, i, j] + cross_ref[p, i, j] for p in range(parts))
                    at = slice(k % half * TILE, (k % half + 1) * TILE)
                    outs[k // half][at, :] = tile + sum(cross_ref[p, j, i] for p in range(parts)).T

        for store in stores:
            store.wait()

    outs = [shape(half * TILE, TILE)] * 2 + [shape(count, width) for _, count in (*pieces, *kept)]
    scratch = [
        pltpu.VMEM((rows, width), F32),
        *[pltpu.VMEM((parts, width, width), F32)] * 2,
        pltpu.SemaphoreType.DMA((parts,)),
        pltpu.SemaphoreType.DMA((len(outs) - 2,)),
    ]
    specs = [IN_VMEM] * 2 + [ANYWHERE] * len(pieces) + [IN_VMEM] * len(kept)
    return call(kernel, "gram", (core, b), [IN_SMEM, ANYWHERE], outs, specs, scratch, after, 57, LONG)


def add(a, b, after):
    def kernel(a_ref, b_ref, out_ref):
        out_ref[...] = a_ref[...] + b_ref[...]

    return call(kernel, "add", (a, b), [IN_VMEM] * 2, shape(*a.shape), IN_VMEM, after=after, vmem=8)


def add_and_cut(second, a, b, after):
    n = a.shape[0] // 2

    def kernel(second_ref, a_ref, b_ref, out_ref, part_ref):
        out_ref[...] = a_ref[...] + b_ref[...]
        for flag, at in ((0, slice(0, n)), (1, slice(n, 2 * n))):

            @pl.when(second_ref[0] == flag)
            def _():
                part_ref[...] = a_ref[at, :] + b_ref[at, :]

    outs = [shape(*a.shape), shape(n, a.shape[1])]
    specs = [IN_SMEM, IN_VMEM, IN_VMEM]
    return call(kernel, "add", (second, a, b), specs, outs, [IN_VMEM] * 2, after=after, vmem=8)


def merge_kernel(second_ref, a_ref, b_ref, out_ref):
    n = a_ref.shape[0]
    for flag, (x_ref, y_ref) in enumerate(((a_ref, b_ref), (b_ref, a_ref))):

        @pl.when(second_ref[0] == flag)
        def _():
            out_ref[:n] = x_ref[...]
            out_ref[n:] = y_ref[...]


def merge(second, a, b, after):
    out = shape(2 * a.shape[0], a.shape[1])
    return call(merge_kernel, "merge", (second, a, b), [IN_SMEM, IN_VMEM, IN_VMEM], out, IN_VMEM, after=after, vmem=8)


def polar_kernel(at_ref, mine_ref, other_ref, high_ref, low_ref, x_ref, one_ref, two_ref):
    width = x_ref.shape[0]
    half = width // 2
    core, top_id, bottom_id, swapped = (at_ref[i] for i in range(4))
    tiles = upper_tiles(width)
    for k, (i, j) in tiles:
        per = len(tiles) // 2
        at = slice(k % per * TILE, (k % per + 1) * TILE)
        tile = jnp.where(core == k // per, mine_ref[at], other_ref[at])
        one_ref[i, j] = tile
        if i != j:
            one_ref[j, i] = tile.T
    row = lax.broadcasted_iota(jnp.int32, (width, width), 0)
    column = lax.broadcasted_iota(jnp.int32, (width, width), 1)
    on_diagonal = row == column

    def global_id(c):
        return jnp.where(c < half, top_id * half + c, bottom_id * half + c - half)

    row_id = global_id(lax.broadcasted_iota(jnp.int32, (width, 1), 0))
    column_id = global_id(lax.broadcasted_iota(jnp.int32, (1, width), 1))
    gram_full = one_ref[...]
    diagonal = jnp.where(on_diagonal, gram_full, 0.0)
    across = jnp.sum(diagonal, axis=0, keepdims=True)
    down = jnp.sum(diagonal, axis=1, keepdims=True)
    skew = gram_full / (down + across + epsilon)
    skew = jnp.where(column_id > row_id, skew, jnp.where(column_id < row_id, -skew, 0.0))
    norm = jnp.sqrt(1.0 + jnp.sum(skew * skew))
    x_ref[...] = (jnp.where(on_diagonal, 1.0, 0.0) + skew) / norm
    for _ in range(STEPS):
        high, low = split(x_ref[...])
        one_ref[...] = inner(high, high)
        two_ref[...] = inner(high, low)
        square = one_ref[...] + two_ref[...] + two_ref[...].T
        turn_high, turn_low = split(jnp.where(on_diagonal, 1.5, 0.0) - 0.5 * square)
        x_ref[...] = product(high, turn_high)
        one_ref[...] = product(high, turn_low)
        two_ref[...] = product(low, turn_high)
        x_ref[...] = x_ref[...] + (one_ref[...] + two_ref[...])
    for flag, (first, second) in enumerate((((0, half), (half, width)), ((half, width), (0, half)))):

        @pl.when(swapped == flag)
        def _():
            for to, (begin, end) in ((0, first), (half, second)):
                high, low = split(x_ref[:, begin:end])
                high_ref[:, to : to + half] = high
                low_ref[:, to : to + half] = low


def polar(at, mine, other, width, after=()):
    specs = [IN_SMEM, IN_VMEM, IN_VMEM]
    outs = [shape(width, width, dtype=BF16)] * 2
    scratch = [pltpu.VMEM((width, width), F32)] * 3
    return call(polar_kernel, "polar", (at, mine, other), specs, outs, [IN_VMEM] * 2, scratch, after, 24, LONG)


def times(rows, w_high, w_low):
    high, low = split(rows)
    return product(high, w_high) + product(high, w_low) + product(low, w_high)


def turn(arrays, w, after=(), spec=WHOLE):
    width = w[0].shape[0]
    half = width // 2

    def kernel(*refs):
        (high_ref, low_ref), parts, outs = refs[:2], refs[2:-2], refs[-2:]
        begin = 0
        for b_ref in parts:
            rows = pl.ds(begin, b_ref.shape[0])
            for out_ref, at in zip(outs, (slice(0, half), slice(half, width)), strict=True):
                out_ref[rows, :] = times(b_ref[...], high_ref[:, at], low_ref[:, at])
            begin += b_ref.shape[0]

    outs = [shape(sum(b.shape[0] for b in arrays), half)] * 2
    return call(kernel, "turn", (*w, *arrays), [WHOLE] * 2 + [spec] * len(arrays), outs, [WHOLE] * 2, after=after, vmem=24)


def take(b, start, count, parts=4):
    rows = count // parts

    def kernel(b_ref, out_ref, sem):
        copies = [
            pltpu.make_async_copy(
                b_ref.at[pl.ds(start + p * rows, rows)], out_ref.at[pl.ds(p * rows, rows)], sem.at[p]
            )
            for p in range(parts)
        ]
        for copy in copies:
            copy.start()
        for copy in copies:
            copy.wait()

    scratch = [pltpu.SemaphoreType.DMA((parts,))]
    return call(kernel, "take", (b,), [ANYWHERE], shape(count, b.shape[1]), IN_VMEM, scratch)


def own(at_end, b, start, count, w, after=()):
    width = b.shape[1]
    half = width // 2

    def kernel(at_end_ref, b_ref, high_ref, low_ref, out_ref, rows_ref, sem):
        @pl.when(at_end_ref[0] == 1)
        def _():
            load = pltpu.make_async_copy(b_ref.at[pl.ds(start, count)], rows_ref, sem)
            load.start()
            load.wait()
            out_ref[...] = times(rows_ref[...], high_ref[:, half:], low_ref[:, half:])

    specs = [IN_SMEM, ANYWHERE, WHOLE, WHOLE]
    scratch = [pltpu.VMEM((count, width), F32), pltpu.SemaphoreType.DMA]
    return call(kernel, "own", (at_end, b, *w), specs, shape(count, half), IN_VMEM, scratch, after, 24)


def join(choice, groups, rows, width, into=None, after=()):
    places = []
    for start, count, sources in groups:
        for s, source in enumerate(sources):
            if source is not None:
                array, begin = source if isinstance(source, tuple) else (source, 0)
                places.append((start, count, s, array, begin))
    half = width // 2

    def kernel(choice_ref, *refs):
        out_ref, sem = refs[-2:]

        def each(act):
            for k, (start, count, s, _, begin) in enumerate(places):
                for side in (0, 1):
                    store = pltpu.make_async_copy(
                        refs[k].at[pl.ds(begin, count)],
                        out_ref.at[pl.ds(start, count), pl.ds(side * half, half)],
                        sem.at[k],
                    )

                    @pl.when(choice_ref[side] == s)
                    def _():
                        act(store)

        each(lambda store: store.start())
        each(lambda store: store.wait())

    operands = (choice, *[array for _, _, _, array, _ in places])
    specs = [IN_SMEM] + [IN_VMEM] * len(places)
    more = {}
    if into is not None:
        more["input_output_aliases"] = {len(operands): 0}
        operands += (into,)
        specs.append(ANYWHERE)
    scratch = [pltpu.SemaphoreType.DMA((len(places),))]
    return call(kernel, "join", operands, specs, shape(rows, width), ANYWHERE, scratch, after, 8, **more)


def mark(after):
    def kernel(out_ref):
        out_ref[...] = jnp.zeros_like(out_ref)

    return call(kernel, "mark", (), [], shape(8, TILE), WHOLE, after=(after,))


def shards(history, round_index):
    rows, width = history.shape
    pairs = lax.axis_size("pair")
    levels = pairs // 2
    position = lax.axis_index("pair")
    partner = position ^ 1
    even = position % 2 == 0
    first, last = position == 0, position == pairs - 1
    core, row_half = lax.axis_index("tm") % 2, lax.axis_index("tm") // 2
    cycle_len = 2 * pairs - 1
    round_now = round_index[0]
    swap_pairs = [(p, p ^ 1) for p in range(pairs)]
    swap_cores = [(i, i ^ 1) for i in range(4)]
    swap_rows = [(i, i ^ 2) for i in range(4)]

    def ids(p):
        top_id = jnp.where(p == 0, 0, 1 + jnp.mod(p - 1 - round_now, cycle_len))
        bottom_id = 1 + jnp.mod(2 * pairs - 2 - p - round_now, cycle_len)
        return top_id, bottom_id

    def is_early(p, threshold):
        level = p // 2
        return (p % 2 == 0) & (level >= threshold) | (p % 2 == 1) & (level <= levels - 1 - threshold)

    groups, pieces = [], []
    begin = 0
    for quarter, parts in PLAN:
        counts = [rows * part // 64 for part in parts]
        groups.append((begin, sum(counts), quarter * levels // 4))
        pieces.append([(begin + sum(counts[:i]), count) for i, count in enumerate(counts)])
        begin += sum(counts)
    early = [k for k, group in enumerate(groups) if group[2] < levels]

    def sent_early(k, rows_of_k):
        return lax.ppermute(rows_of_k, "pair", [(p, p ^ 1) for p in range(pairs) if is_early(p, groups[k][2])])

    from_partner = {k: [] for k in early}
    taken = [history[begin : begin + count] for begin, count in pieces[early[0]]]
    from_partner[early[0]] = [sent_early(early[0], a) for a in taken]

    later = [(k, piece) for k in early[1:] for piece in pieces[k]]
    kept = [k for k in range(len(groups)) if groups[k][2] > 0]
    at_once, then = [piece for _, piece in later], [groups[k][:2] for k in kept]
    keep, give, *copies = gram(jnp.stack([core]), history, at_once, then, taken)
    kept = dict(zip(kept, copies[len(later) :]))
    summed = add(keep, lax.ppermute(give, "tm", swap_cores), from_partner[early[0]][:1])
    from_row = lax.ppermute(summed, "tm", swap_rows)
    second = jnp.stack([row_half])
    mine, part = add_and_cut(second, summed, from_row, ())
    other = lax.ppermute(mine, "tm", swap_cores)
    part = lax.ppermute(part, "pair", swap_pairs)
    for (k, _), a in zip(later, copies):
        from_partner[k].append(sent_early(k, a))

    flag = (~even | first).astype(jnp.int32)
    w = polar(jnp.stack([core, *ids(position), flag]), mine, other, width, (part, *from_partner[early[0]]))
    late = {}
    for k, (_, _, threshold) in enumerate(groups):
        if threshold > 0:
            near, far = turn([kept[k]], w, spec=IN_VMEM)
            to_partner = [(p, p ^ 1) for p in range(pairs) if not is_early(p, threshold)]
            onward = [(p, p - 1) for p in range(2, pairs, 2) if not is_early(p, threshold)]
            onward += [(p, p + 1) for p in range(1, pairs - 1, 2) if not is_early(p, threshold)]
            late[k] = lax.ppermute(near, "pair", to_partner), lax.ppermute(far, "pair", onward), far

    part_2 = lax.ppermute(part, "tm", swap_rows)
    mine_q = merge(second, part, part_2, [late[k][2] for k in late])
    other_q = lax.ppermute(mine_q, "tm", swap_cores)
    flag_q = (even | (partner == 0)).astype(jnp.int32)
    w_q = polar(jnp.stack([core, *ids(partner), flag_q]), mine_q, other_q, width, from_partner[early[1]])
    at_end = jnp.stack([first | last]).astype(jnp.int32)
    near, passed = {}, {}
    always = [k for k in early if groups[k][2] == 0]
    after = ()
    for k in early:
        threshold = groups[k][2]
        near[k], far = turn(from_partner[k], w_q, after)
        onward = [(p ^ 1, p - 1) for p in range(2, pairs, 2) if is_early(p, threshold)]
        onward += [(p ^ 1, p + 1) for p in range(1, pairs - 1, 2) if is_early(p, threshold)]
        passed[k] = lax.ppermute(far, "pair", onward)
        if k == early[0]:
            alone = own(at_end, history, groups[always[0]][0], sum(groups[k][1] for k in always), w, (far,))
            after = (alone,)

    sources = {k: (near[k], passed[k], (alone, groups[k][0])) for k in early} | late
    choice = jnp.stack([jnp.where(even, 1 + first, 0), jnp.where(even, 0, 1 + last)]).astype(jnp.int32)
    near_late = {k: (sources[k][0], None, None) for k in late}
    far_late = {k: (None, *sources[k][1:]) for k in late}
    first_part, last_part = {k: sources[k] for k in early} | far_late, near_late
    joined = join(choice, [(*groups[k][:2], first_part[k]) for k in first_part], rows, width)
    last_groups = [(*groups[k][:2], last_part[k]) for k in last_part]
    return join(choice, last_groups, rows, width, joined, (mark(joined),))


def solution(mesh):
    in_specs = (P("tm", "pair"), P())
    out_specs = P("tm", "pair")
    return jax.shard_map(shards, mesh=mesh, in_specs=in_specs, out_specs=out_specs, check_vma=False)
```

```python
import jax
import jax.numpy as jnp
from jax import lax
from jax.experimental import pallas as pl
from jax.experimental.pallas import tpu as pltpu
from jax.sharding import PartitionSpec as P

STEPS = 4
TILE = 128
F32, BF16 = jnp.float32, jnp.bfloat16

epsilon = 1e-06

PLAN = ((0, (6, 12, 13)), (4, (33,)))
FIRST = 2

MIB = 1 << 20
LONG = 10**12
WHOLE = pl.BlockSpec()
IN_VMEM = pl.BlockSpec(memory_space=pltpu.VMEM)
IN_SMEM = pl.BlockSpec(memory_space=pltpu.SMEM)
ANYWHERE = pl.BlockSpec(memory_space=pl.ANY)
IN_HBM = pl.BlockSpec(memory_space=pltpu.HBM)


def call(kernel, name, operands, in_specs, outs, out_specs, scratch=(), after=(), vmem=56, flops=0, after_spec=ANYWHERE, **more):
    given, late = len(operands), len(after)

    def body(*refs):
        kernel(*refs[:given], *refs[given + late :])

    return pl.pallas_call(
        body,
        in_specs=[*in_specs, *[after_spec] * late],
        out_specs=out_specs,
        out_shape=outs,
        scratch_shapes=scratch,
        compiler_params=pltpu.CompilerParams(vmem_limit_bytes=vmem * MIB),
        cost_estimate=pl.CostEstimate(flops=flops, bytes_accessed=0, transcendentals=0),
        name=name,
        **more,
    )(*operands, *after)


def shape(*dims, dtype=F32):
    return jax.ShapeDtypeStruct(dims, dtype)


def split(x):
    high = x.astype(BF16)
    return high, (x - high.astype(F32)).astype(BF16)


def product(a, b):
    return jnp.dot(a, b, preferred_element_type=F32)


def inner(a, b):
    return lax.dot_general(a, b, (((0,), (0,)), ((), ())), preferred_element_type=F32)


def upper_tiles(width):
    n = width // TILE
    at = [slice(i * TILE, (i + 1) * TILE) for i in range(n)]
    return list(enumerate((at[i], at[j]) for i in range(n) for j in range(i, n)))


def gram(core, b, pieces, kept, after, parts=4):
    rows, width = b.shape
    tiles = upper_tiles(width)
    half = len(tiles) // 2

    def kernel(core_ref, b_ref, *refs):
        mine_ref, other_ref, *copies = refs[:-5]
        rows_ref, high_ref, cross_ref, load_sem, store_sem = refs[-5:]
        loads = [
            pltpu.make_async_copy(b_ref.at[pl.ds(p * (rows // parts), rows // parts)], at, load_sem.at[p])
            for p, at in enumerate(rows_ref.at[pl.ds(p * (rows // parts), rows // parts)] for p in range(parts))
        ]
        stores = [
            pltpu.make_async_copy(rows_ref.at[pl.ds(*piece)], copies[k], store_sem.at[k])
            for k, piece in enumerate((*pieces, *kept))
        ]
        for load in loads:
            load.start()
        for p, load in enumerate(loads):
            load.wait()
            high, low = split(rows_ref[p * (rows // parts) : (p + 1) * (rows // parts)])
            high_ref[p] = inner(high, high)
            cross_ref[p] = inner(high, low)
        for store in stores:
            store.start()

        for flag, outs in enumerate(((mine_ref, other_ref), (other_ref, mine_ref))):

            @pl.when(core_ref[0] == flag)
            def _():
                for k, (i, j) in tiles:
                    tile = sum(high_ref[p, i, j] + cross_ref[p, i, j] for p in range(parts))
                    at = slice(k % half * TILE, (k % half + 1) * TILE)
                    outs[k // half][at, :] = tile + sum(cross_ref[p, j, i] for p in range(parts)).T

        for store in stores:
            store.wait()

    outs = [shape(half * TILE, TILE)] * 2 + [shape(count, width) for _, count in (*pieces, *kept)]
    scratch = [
        pltpu.VMEM((rows, width), F32),
        *[pltpu.VMEM((parts, width, width), F32)] * 2,
        pltpu.SemaphoreType.DMA((parts,)),
        pltpu.SemaphoreType.DMA((len(outs) - 2,)),
    ]
    specs = [IN_VMEM] * 2 + [ANYWHERE] * len(pieces) + [IN_VMEM] * len(kept)
    return call(kernel, "gram", (core, b), [IN_SMEM, ANYWHERE], outs, specs, scratch, after, 57, LONG)


def add(a, b, after):
    def kernel(a_ref, b_ref, out_ref):
        out_ref[...] = a_ref[...] + b_ref[...]

    return call(kernel, "add", (a, b), [IN_VMEM] * 2, shape(*a.shape), IN_VMEM, after=after, vmem=8)


def add_and_cut(second, a, b, after):
    n = a.shape[0] // 2

    def kernel(second_ref, a_ref, b_ref, out_ref, part_ref):
        out_ref[...] = a_ref[...] + b_ref[...]
        for flag, at in ((0, slice(0, n)), (1, slice(n, 2 * n))):

            @pl.when(second_ref[0] == flag)
            def _():
                part_ref[...] = a_ref[at, :] + b_ref[at, :]

    outs = [shape(*a.shape), shape(n, a.shape[1])]
    specs = [IN_SMEM, IN_VMEM, IN_VMEM]
    return call(kernel, "add", (second, a, b), specs, outs, [IN_VMEM] * 2, after=after, vmem=8)


def merge_kernel(second_ref, a_ref, b_ref, out_ref):
    n = a_ref.shape[0]
    for flag, (x_ref, y_ref) in enumerate(((a_ref, b_ref), (b_ref, a_ref))):

        @pl.when(second_ref[0] == flag)
        def _():
            out_ref[:n] = x_ref[...]
            out_ref[n:] = y_ref[...]


def merge(second, a, b, after):
    out = shape(2 * a.shape[0], a.shape[1])
    return call(merge_kernel, "merge", (second, a, b), [IN_SMEM, IN_VMEM, IN_VMEM], out, IN_VMEM, after=after, vmem=8)


def polar_kernel(at_ref, mine_ref, other_ref, high_ref, low_ref, x_ref, one_ref, two_ref):
    width = x_ref.shape[0]
    half = width // 2
    core, top_id, bottom_id, swapped = (at_ref[i] for i in range(4))
    tiles = upper_tiles(width)
    for k, (i, j) in tiles:
        per = len(tiles) // 2
        at = slice(k % per * TILE, (k % per + 1) * TILE)
        tile = jnp.where(core == k // per, mine_ref[at], other_ref[at])
        one_ref[i, j] = tile
        if i != j:
            one_ref[j, i] = tile.T
    row = lax.broadcasted_iota(jnp.int32, (width, width), 0)
    column = lax.broadcasted_iota(jnp.int32, (width, width), 1)
    on_diagonal = row == column

    def global_id(c):
        return jnp.where(c < half, top_id * half + c, bottom_id * half + c - half)

    row_id = global_id(lax.broadcasted_iota(jnp.int32, (width, 1), 0))
    column_id = global_id(lax.broadcasted_iota(jnp.int32, (1, width), 1))
    gram_full = one_ref[...]
    diagonal = jnp.where(on_diagonal, gram_full, 0.0)
    across = jnp.sum(diagonal, axis=0, keepdims=True)
    down = jnp.sum(diagonal, axis=1, keepdims=True)
    skew = gram_full / (down + across + epsilon)
    skew = jnp.where(column_id > row_id, skew, jnp.where(column_id < row_id, -skew, 0.0))
    norm = jnp.sqrt(1.0 + jnp.sum(skew * skew))
    x_ref[...] = (jnp.where(on_diagonal, 1.0, 0.0) + skew) / norm
    for _ in range(STEPS):
        high, low = split(x_ref[...])
        one_ref[...] = inner(high, high)
        two_ref[...] = inner(high, low)
        square = one_ref[...] + two_ref[...] + two_ref[...].T
        turn_high, turn_low = split(jnp.where(on_diagonal, 1.5, 0.0) - 0.5 * square)
        x_ref[...] = product(high, turn_high)
        one_ref[...] = product(high, turn_low)
        two_ref[...] = product(low, turn_high)
        x_ref[...] = x_ref[...] + (one_ref[...] + two_ref[...])
    for flag, (first, second) in enumerate((((0, half), (half, width)), ((half, width), (0, half)))):

        @pl.when(swapped == flag)
        def _():
            for to, (begin, end) in ((0, first), (half, second)):
                high, low = split(x_ref[:, begin:end])
                high_ref[:, to : to + half] = high
                low_ref[:, to : to + half] = low


def polar(at, mine, other, width, after=()):
    specs = [IN_SMEM, IN_VMEM, IN_VMEM]
    outs = [shape(width, width, dtype=BF16)] * 2
    scratch = [pltpu.VMEM((width, width), F32)] * 3
    return call(polar_kernel, "polar", (at, mine, other), specs, outs, [IN_VMEM] * 2, scratch, after, 24, LONG, IN_HBM)


def times(rows, w_high, w_low):
    high, low = split(rows)
    return product(high, w_high) + product(high, w_low) + product(low, w_high)


def turn(arrays, w, wanted, after=(), spec=WHOLE):
    half = w[0].shape[0] // 2

    def kernel(*refs):
        (high_ref, low_ref), parts, outs = refs[:2], refs[2 : 2 + len(arrays)], refs[2 + len(arrays) :]
        for out_ref, (side, begin, end) in zip(outs, wanted):
            columns = slice(side * half, (side + 1) * half)
            w_high, w_low = high_ref[:, columns], low_ref[:, columns]
            at = 0
            for b_ref in parts:
                size = b_ref.shape[0]
                lower, upper = max(begin, at), min(end, at + size)
                if lower < upper:
                    out_ref[lower - begin : upper - begin, :] = times(b_ref[lower - at : upper - at, :], w_high, w_low)
                at += size

    outs = [shape(end - begin, half) for _, begin, end in wanted]
    specs = [WHOLE] * 2 + [spec] * len(arrays)
    return call(kernel, "turn", (*w, *arrays), specs, outs, [WHOLE] * len(outs), after=after, vmem=24)


def own(at_end, b, start, count, w, after=()):
    width = b.shape[1]
    half = width // 2

    def kernel(at_end_ref, b_ref, high_ref, low_ref, out_ref, rows_ref, sem):
        @pl.when(at_end_ref[0] == 1)
        def _():
            load = pltpu.make_async_copy(b_ref.at[pl.ds(start, count)], rows_ref, sem)
            load.start()
            load.wait()
            out_ref[...] = times(rows_ref[...], high_ref[:, half:], low_ref[:, half:])

    specs = [IN_SMEM, ANYWHERE, WHOLE, WHOLE]
    scratch = [pltpu.VMEM((count, width), F32), pltpu.SemaphoreType.DMA]
    return call(kernel, "own", (at_end, b, *w), specs, shape(count, half), IN_VMEM, scratch, after, 24)


def join(choice, groups, rows, width, into=None, token=None, vmem=8):
    places = []
    for start, count, sources in groups:
        for s, source in enumerate(sources):
            if source is not None:
                array, begin = source if isinstance(source, tuple) else (source, 0)
                places.append((start, count, s, array, begin))
    half = width // 2

    def kernel(choice_ref, *refs):
        out_ref, sem = refs[-2:]

        def each(act):
            for k, (start, count, s, _, begin) in enumerate(places):
                for side in (0, 1):
                    store = pltpu.make_async_copy(
                        refs[k].at[pl.ds(begin, count)],
                        out_ref.at[pl.ds(start, count), pl.ds(side * half, half)],
                        sem.at[k],
                    )

                    @pl.when(choice_ref[side] == s)
                    def _():
                        act(store)

        each(lambda store: store.start())
        each(lambda store: store.wait())

    operands = (choice, *[array for _, _, _, array, _ in places])
    specs = [IN_SMEM] + [IN_VMEM] * len(places)
    more = {}
    if into is not None:
        more["input_output_aliases"] = {len(operands): 0}
        operands += (into, token)
        specs += [ANYWHERE, ANYWHERE]
    scratch = [pltpu.SemaphoreType.DMA((len(places),))]
    return call(kernel, "join", operands, specs, shape(rows, width), ANYWHERE, scratch, vmem=vmem, **more)


def mark(after):
    def kernel(out_ref):
        out_ref[...] = jnp.zeros_like(out_ref)

    return call(kernel, "mark", (), [], shape(8, TILE), WHOLE, after=(after,))


def shards(history, round_index):
    rows, width = history.shape
    pairs = lax.axis_size("pair")
    levels = pairs // 2
    position = lax.axis_index("pair")
    partner = position ^ 1
    even = position % 2 == 0
    first, last = position == 0, position == pairs - 1
    core, row_half = lax.axis_index("tm") % 2, lax.axis_index("tm") // 2
    cycle_len = 2 * pairs - 1
    round_now = round_index[0]
    swap_pairs = [(p, p ^ 1) for p in range(pairs)]
    swap_cores = [(i, i ^ 1) for i in range(4)]
    swap_rows = [(i, i ^ 2) for i in range(4)]

    def ids(p):
        top_id = jnp.where(p == 0, 0, 1 + jnp.mod(p - 1 - round_now, cycle_len))
        bottom_id = 1 + jnp.mod(2 * pairs - 2 - p - round_now, cycle_len)
        return top_id, bottom_id

    def is_early(p, threshold):
        level = p // 2
        return (p % 2 == 0) & (level >= threshold) | (p % 2 == 1) & (level <= levels - 1 - threshold)

    groups, pieces = [], []
    begin = 0
    for quarter, parts in PLAN:
        counts = [rows * part // 64 for part in parts]
        groups.append((begin, sum(counts), quarter * levels // 4))
        pieces.append([(begin + sum(counts[:i]), count) for i, count in enumerate(counts)])
        begin += sum(counts)
    early = [k for k, group in enumerate(groups) if group[2] < levels]

    def sent_early(k, rows_of_k):
        return lax.ppermute(rows_of_k, "pair", [(p, p ^ 1) for p in range(pairs) if is_early(p, groups[k][2])])

    (e,) = early
    taken = [history[begin : begin + count] for begin, count in pieces[e][:FIRST]]
    from_partner = [sent_early(e, a) for a in taken]

    kept = [k for k in range(len(groups)) if groups[k][2] > 0]
    later = pieces[e][FIRST:]
    keep, give, *copies = gram(jnp.stack([core]), history, later, [groups[k][:2] for k in kept], taken)
    kept = dict(zip(kept, copies[len(later) :]))
    summed = add(keep, lax.ppermute(give, "tm", swap_cores), from_partner[:1])
    from_row = lax.ppermute(summed, "tm", swap_rows)
    second = jnp.stack([row_half])
    mine, part = add_and_cut(second, summed, from_row, ())
    other = lax.ppermute(mine, "tm", swap_cores)
    part = lax.ppermute(part, "pair", swap_pairs)
    from_partner += [sent_early(e, a) for a in copies[: len(later)]]

    flag = (~even | first).astype(jnp.int32)
    w = polar(jnp.stack([core, *ids(position), flag]), mine, other, width, (part, *from_partner[:FIRST]))
    to_partner, onward = {}, {}
    for k, (_, _, threshold) in enumerate(groups):
        to_partner[k] = [(p, p ^ 1) for p in range(pairs) if not is_early(p, threshold)]
        onward[k] = [(p, p - 1) for p in range(2, pairs, 2) if not is_early(p, threshold)]
        onward[k] += [(p, p + 1) for p in range(1, pairs - 1, 2) if not is_early(p, threshold)]
    late_near, late_far = {}, {}
    for k in kept:
        count = groups[k][1]
        (a,) = turn([kept[k]], w, [(0, 0, count)], spec=IN_VMEM)
        late_near[k] = a, lax.ppermute(a, "pair", to_partner[k])
        cut = count // 32 * 16
        both = turn([kept[k]], w, [(1, 0, cut), (1, cut, count)], [a], IN_VMEM)
        late_far[k] = [(at, a, lax.ppermute(a, "pair", onward[k])) for at, a in zip((0, cut), both)]

    part_2 = lax.ppermute(part, "tm", swap_rows)
    mine_q = merge(second, part, part_2, [late_far[k][0][1] for k in kept])
    other_q = lax.ppermute(mine_q, "tm", swap_cores)
    flag_q = (even | (partner == 0)).astype(jnp.int32)
    w_q = polar(jnp.stack([core, *ids(partner), flag_q]), mine_q, other_q, width, from_partner[FIRST:])
    at_end = jnp.stack([first | last]).astype(jnp.int32)
    begin, count, threshold = groups[e]
    near, far = turn(from_partner, w_q, [(0, 0, count), (1, 0, count)])
    passes = [(p ^ 1, p - 1) for p in range(2, pairs, 2) if is_early(p, threshold)]
    passes += [(p ^ 1, p + 1) for p in range(1, pairs - 1, 2) if is_early(p, threshold)]
    passed = lax.ppermute(far, "pair", passes)
    alone = own(at_end, history, begin, count, w, (far,))

    choice = jnp.stack([jnp.where(even, 1 + first, 0), jnp.where(even, 0, 1 + last)]).astype(jnp.int32)
    parts = [[(begin, count, (near, None, alone))], [(begin, count, (None, passed, None))], []]
    for k in kept:
        begin, count = groups[k][:2]
        for at, a, from_far in late_far[k]:
            parts[1].append((begin + at, a.shape[0], (None, from_far, a)))
        parts[2].append((begin, count, (late_near[k][1], None, None)))
    joined = join(choice, parts[0], rows, width)
    for part in parts[1:]:
        joined = join(choice, part, rows, width, joined, mark(joined), 56)
    return joined


def solution(mesh):
    in_specs = (P("tm", "pair"), P())
    out_specs = P("tm", "pair")
    return jax.shard_map(shards, mesh=mesh, in_specs=in_specs, out_specs=out_specs, check_vma=False)
```

```python
import jax
import jax.numpy as jnp
from jax import lax
from jax.experimental import pallas as pl
from jax.experimental.pallas import tpu as pltpu
from jax.sharding import PartitionSpec as P

STEPS = 4
TILE = 128
F32, BF16 = jnp.float32, jnp.bfloat16

epsilon = 1e-06

PLAN = ((0, (6, 12, 13)), (4, (33,)))
FIRST, LAST = 2, 6

MIB = 1 << 20
LONG = 10**12
WHOLE = pl.BlockSpec()
IN_VMEM = pl.BlockSpec(memory_space=pltpu.VMEM)
IN_SMEM = pl.BlockSpec(memory_space=pltpu.SMEM)
ANYWHERE = pl.BlockSpec(memory_space=pl.ANY)
IN_HBM = pl.BlockSpec(memory_space=pltpu.HBM)


def call(kernel, name, operands, in_specs, outs, out_specs, scratch=(), after=(), vmem=56, flops=0, after_spec=ANYWHERE, **more):
    given, late = len(operands), len(after)

    def body(*refs):
        kernel(*refs[:given], *refs[given + late :])

    return pl.pallas_call(
        body,
        in_specs=[*in_specs, *[after_spec] * late],
        out_specs=out_specs,
        out_shape=outs,
        scratch_shapes=scratch,
        compiler_params=pltpu.CompilerParams(vmem_limit_bytes=vmem * MIB),
        cost_estimate=pl.CostEstimate(flops=flops, bytes_accessed=0, transcendentals=0),
        name=name,
        **more,
    )(*operands, *after)


def shape(*dims, dtype=F32):
    return jax.ShapeDtypeStruct(dims, dtype)


def split(x):
    high = x.astype(BF16)
    return high, (x - high.astype(F32)).astype(BF16)


def product(a, b):
    return jnp.dot(a, b, preferred_element_type=F32)


def inner(a, b):
    return lax.dot_general(a, b, (((0,), (0,)), ((), ())), preferred_element_type=F32)


def upper_tiles(width):
    n = width // TILE
    at = [slice(i * TILE, (i + 1) * TILE) for i in range(n)]
    return list(enumerate((at[i], at[j]) for i in range(n) for j in range(i, n)))


def gram(core, b, pieces, kept, after, parts=4):
    rows, width = b.shape
    tiles = upper_tiles(width)
    half = len(tiles) // 2

    def kernel(core_ref, b_ref, *refs):
        mine_ref, other_ref, *copies = refs[:-5]
        rows_ref, high_ref, cross_ref, load_sem, store_sem = refs[-5:]
        loads = [
            pltpu.make_async_copy(b_ref.at[pl.ds(p * (rows // parts), rows // parts)], at, load_sem.at[p])
            for p, at in enumerate(rows_ref.at[pl.ds(p * (rows // parts), rows // parts)] for p in range(parts))
        ]
        stores = [
            pltpu.make_async_copy(rows_ref.at[pl.ds(*piece)], copies[k], store_sem.at[k])
            for k, piece in enumerate((*pieces, *kept))
        ]
        for load in loads:
            load.start()
        for p, load in enumerate(loads):
            load.wait()
            high, low = split(rows_ref[p * (rows // parts) : (p + 1) * (rows // parts)])
            high_ref[p] = inner(high, high)
            cross_ref[p] = inner(high, low)
        for store in stores:
            store.start()

        for flag, outs in enumerate(((mine_ref, other_ref), (other_ref, mine_ref))):

            @pl.when(core_ref[0] == flag)
            def _():
                for k, (i, j) in tiles:
                    tile = sum(high_ref[p, i, j] + cross_ref[p, i, j] for p in range(parts))
                    at = slice(k % half * TILE, (k % half + 1) * TILE)
                    outs[k // half][at, :] = tile + sum(cross_ref[p, j, i] for p in range(parts)).T

        for store in stores:
            store.wait()

    outs = [shape(half * TILE, TILE)] * 2 + [shape(count, width) for _, count in (*pieces, *kept)]
    scratch = [
        pltpu.VMEM((rows, width), F32),
        *[pltpu.VMEM((parts, width, width), F32)] * 2,
        pltpu.SemaphoreType.DMA((parts,)),
        pltpu.SemaphoreType.DMA((len(outs) - 2,)),
    ]
    specs = [IN_VMEM] * 2 + [ANYWHERE] * len(pieces) + [IN_VMEM] * len(kept)
    return call(kernel, "gram", (core, b), [IN_SMEM, ANYWHERE], outs, specs, scratch, after, 57, LONG)


def add(a, b, after):
    def kernel(a_ref, b_ref, out_ref):
        out_ref[...] = a_ref[...] + b_ref[...]

    return call(kernel, "add", (a, b), [IN_VMEM] * 2, shape(*a.shape), IN_VMEM, after=after, vmem=8)


def add_and_cut(second, a, b, after):
    n = a.shape[0] // 2

    def kernel(second_ref, a_ref, b_ref, out_ref, part_ref):
        out_ref[...] = a_ref[...] + b_ref[...]
        for flag, at in ((0, slice(0, n)), (1, slice(n, 2 * n))):

            @pl.when(second_ref[0] == flag)
            def _():
                part_ref[...] = a_ref[at, :] + b_ref[at, :]

    outs = [shape(*a.shape), shape(n, a.shape[1])]
    specs = [IN_SMEM, IN_VMEM, IN_VMEM]
    return call(kernel, "add", (second, a, b), specs, outs, [IN_VMEM] * 2, after=after, vmem=8)


def merge_kernel(second_ref, a_ref, b_ref, out_ref):
    n = a_ref.shape[0]
    for flag, (x_ref, y_ref) in enumerate(((a_ref, b_ref), (b_ref, a_ref))):

        @pl.when(second_ref[0] == flag)
        def _():
            out_ref[:n] = x_ref[...]
            out_ref[n:] = y_ref[...]


def merge(second, a, b, after):
    out = shape(2 * a.shape[0], a.shape[1])
    return call(merge_kernel, "merge", (second, a, b), [IN_SMEM, IN_VMEM, IN_VMEM], out, IN_VMEM, after=after, vmem=8)


def polar_kernel(at_ref, mine_ref, other_ref, high_ref, low_ref, x_ref, one_ref, two_ref):
    width = x_ref.shape[0]
    half = width // 2
    core, top_id, bottom_id, swapped = (at_ref[i] for i in range(4))
    tiles = upper_tiles(width)
    for k, (i, j) in tiles:
        per = len(tiles) // 2
        at = slice(k % per * TILE, (k % per + 1) * TILE)
        tile = jnp.where(core == k // per, mine_ref[at], other_ref[at])
        one_ref[i, j] = tile
        if i != j:
            one_ref[j, i] = tile.T
    row = lax.broadcasted_iota(jnp.int32, (width, width), 0)
    column = lax.broadcasted_iota(jnp.int32, (width, width), 1)
    on_diagonal = row == column

    def global_id(c):
        return jnp.where(c < half, top_id * half + c, bottom_id * half + c - half)

    row_id = global_id(lax.broadcasted_iota(jnp.int32, (width, 1), 0))
    column_id = global_id(lax.broadcasted_iota(jnp.int32, (1, width), 1))
    gram_full = one_ref[...]
    diagonal = jnp.where(on_diagonal, gram_full, 0.0)
    across = jnp.sum(diagonal, axis=0, keepdims=True)
    down = jnp.sum(diagonal, axis=1, keepdims=True)
    skew = gram_full / (down + across + epsilon)
    skew = jnp.where(column_id > row_id, skew, jnp.where(column_id < row_id, -skew, 0.0))
    norm = jnp.sqrt(1.0 + jnp.sum(skew * skew))
    x_ref[...] = (jnp.where(on_diagonal, 1.0, 0.0) + skew) / norm
    for _ in range(STEPS):
        high, low = split(x_ref[...])
        one_ref[...] = inner(high, high)
        two_ref[...] = inner(high, low)
        square = one_ref[...] + two_ref[...] + two_ref[...].T
        turn_high, turn_low = split(jnp.where(on_diagonal, 1.5, 0.0) - 0.5 * square)
        x_ref[...] = product(high, turn_high)
        one_ref[...] = product(high, turn_low)
        two_ref[...] = product(low, turn_high)
        x_ref[...] = x_ref[...] + (one_ref[...] + two_ref[...])
    for flag, (first, second) in enumerate((((0, half), (half, width)), ((half, width), (0, half)))):

        @pl.when(swapped == flag)
        def _():
            for to, (begin, end) in ((0, first), (half, second)):
                high, low = split(x_ref[:, begin:end])
                high_ref[:, to : to + half] = high
                low_ref[:, to : to + half] = low


def polar(at, mine, other, width, after=()):
    specs = [IN_SMEM, IN_VMEM, IN_VMEM]
    outs = [shape(width, width, dtype=BF16)] * 2
    scratch = [pltpu.VMEM((width, width), F32)] * 3
    return call(polar_kernel, "polar", (at, mine, other), specs, outs, [IN_VMEM] * 2, scratch, after, 24, LONG, IN_HBM)


def times(rows, w_high, w_low):
    high, low = split(rows)
    return product(high, w_high) + product(high, w_low) + product(low, w_high)


def turn(arrays, w, wanted, after=(), spec=WHOLE):
    half = w[0].shape[0] // 2

    def kernel(*refs):
        (high_ref, low_ref), parts, outs = refs[:2], refs[2 : 2 + len(arrays)], refs[2 + len(arrays) :]
        for out_ref, (side, begin, end) in zip(outs, wanted):
            columns = slice(side * half, (side + 1) * half)
            w_high, w_low = high_ref[:, columns], low_ref[:, columns]
            at = 0
            for b_ref in parts:
                size = b_ref.shape[0]
                lower, upper = max(begin, at), min(end, at + size)
                if lower < upper:
                    out_ref[lower - begin : upper - begin, :] = times(b_ref[lower - at : upper - at, :], w_high, w_low)
                at += size

    outs = [shape(end - begin, half) for _, begin, end in wanted]
    specs = [WHOLE] * 2 + [spec] * len(arrays)
    return call(kernel, "turn", (*w, *arrays), specs, outs, [WHOLE] * len(outs), after=after, vmem=24)


def own(at_end, b, start, count, w, after=()):
    width = b.shape[1]
    half = width // 2

    def kernel(at_end_ref, b_ref, high_ref, low_ref, out_ref, rows_ref, sem):
        @pl.when(at_end_ref[0] == 1)
        def _():
            load = pltpu.make_async_copy(b_ref.at[pl.ds(start, count)], rows_ref, sem)
            load.start()
            load.wait()
            out_ref[...] = times(rows_ref[...], high_ref[:, half:], low_ref[:, half:])

    specs = [IN_SMEM, ANYWHERE, WHOLE, WHOLE]
    scratch = [pltpu.VMEM((count, width), F32), pltpu.SemaphoreType.DMA]
    return call(kernel, "own", (at_end, b, *w), specs, shape(count, half), IN_VMEM, scratch, after, 24)


def join(choice, groups, rows, width, into=None, token=None, vmem=8):
    places = []
    for start, count, sources in groups:
        for s, source in enumerate(sources):
            if source is not None:
                array, begin = source if isinstance(source, tuple) else (source, 0)
                places.append((start, count, s, array, begin))
    half = width // 2

    def kernel(choice_ref, *refs):
        out_ref, sem = refs[-2:]

        def each(act):
            for k, (start, count, s, _, begin) in enumerate(places):
                for side in (0, 1):
                    store = pltpu.make_async_copy(
                        refs[k].at[pl.ds(begin, count)],
                        out_ref.at[pl.ds(start, count), pl.ds(side * half, half)],
                        sem.at[k],
                    )

                    @pl.when(choice_ref[side] == s)
                    def _():
                        act(store)

        each(lambda store: store.start())
        each(lambda store: store.wait())

    operands = (choice, *[array for _, _, _, array, _ in places])
    specs = [IN_SMEM] + [IN_VMEM] * len(places)
    more = {}
    if into is not None:
        more["input_output_aliases"] = {len(operands): 0}
        operands += (into, token)
        specs += [ANYWHERE, ANYWHERE]
    scratch = [pltpu.SemaphoreType.DMA((len(places),))]
    return call(kernel, "join", operands, specs, shape(rows, width), ANYWHERE, scratch, vmem=vmem, **more)


def mark(after):
    def kernel(out_ref):
        out_ref[...] = jnp.zeros_like(out_ref)

    return call(kernel, "mark", (), [], shape(8, TILE), WHOLE, after=(after,))


def shards(history, round_index):
    rows, width = history.shape
    pairs = lax.axis_size("pair")
    levels = pairs // 2
    position = lax.axis_index("pair")
    partner = position ^ 1
    even = position % 2 == 0
    first, last = position == 0, position == pairs - 1
    core, row_half = lax.axis_index("tm") % 2, lax.axis_index("tm") // 2
    cycle_len = 2 * pairs - 1
    round_now = round_index[0]
    swap_pairs = [(p, p ^ 1) for p in range(pairs)]
    swap_cores = [(i, i ^ 1) for i in range(4)]
    swap_rows = [(i, i ^ 2) for i in range(4)]

    def ids(p):
        top_id = jnp.where(p == 0, 0, 1 + jnp.mod(p - 1 - round_now, cycle_len))
        bottom_id = 1 + jnp.mod(2 * pairs - 2 - p - round_now, cycle_len)
        return top_id, bottom_id

    def is_early(p, threshold):
        level = p // 2
        return (p % 2 == 0) & (level >= threshold) | (p % 2 == 1) & (level <= levels - 1 - threshold)

    groups, pieces = [], []
    begin = 0
    for quarter, parts in PLAN:
        counts = [rows * part // 64 for part in parts]
        groups.append((begin, sum(counts), quarter * levels // 4))
        pieces.append([(begin + sum(counts[:i]), count) for i, count in enumerate(counts)])
        begin += sum(counts)
    early = [k for k, group in enumerate(groups) if group[2] < levels]

    def sent_early(k, rows_of_k):
        return lax.ppermute(rows_of_k, "pair", [(p, p ^ 1) for p in range(pairs) if is_early(p, groups[k][2])])

    (e,) = early
    taken = [history[begin : begin + count] for begin, count in pieces[e][:FIRST]]
    from_partner = [sent_early(e, a) for a in taken]

    kept = [k for k in range(len(groups)) if groups[k][2] > 0]
    later = pieces[e][FIRST:]
    keep, give, *copies = gram(jnp.stack([core]), history, later, [groups[k][:2] for k in kept], taken)
    kept = dict(zip(kept, copies[len(later) :]))
    summed = add(keep, lax.ppermute(give, "tm", swap_cores), from_partner[:1])
    from_row = lax.ppermute(summed, "tm", swap_rows)
    second = jnp.stack([row_half])
    mine, part = add_and_cut(second, summed, from_row, ())
    other = lax.ppermute(mine, "tm", swap_cores)
    part = lax.ppermute(part, "pair", swap_pairs)
    from_partner += [sent_early(e, a) for a in copies[: len(later)]]

    flag = (~even | first).astype(jnp.int32)
    w = polar(jnp.stack([core, *ids(position), flag]), mine, other, width, (part, *from_partner[:FIRST]))
    to_partner, onward = {}, {}
    for k, (_, _, threshold) in enumerate(groups):
        to_partner[k] = [(p, p ^ 1) for p in range(pairs) if not is_early(p, threshold)]
        onward[k] = [(p, p - 1) for p in range(2, pairs, 2) if not is_early(p, threshold)]
        onward[k] += [(p, p + 1) for p in range(1, pairs - 1, 2) if not is_early(p, threshold)]
    late_near, late_far = {}, {}
    for k in kept:
        count = groups[k][1]
        cut = count - rows * LAST // 64
        two = turn([kept[k]], w, [(0, 0, cut), (0, cut, count)], spec=IN_VMEM)
        late_near[k] = [(at, a.shape[0], lax.ppermute(a, "pair", to_partner[k])) for at, a in zip((0, cut), two)]
        cut = count // 32 * 16
        two = turn([kept[k]], w, [(1, 0, cut), (1, cut, count)], two[:1], IN_VMEM)
        late_far[k] = [(at, a, lax.ppermute(a, "pair", onward[k])) for at, a in zip((0, cut), two)]

    part_2 = lax.ppermute(part, "tm", swap_rows)
    mine_q = merge(second, part, part_2, [late_far[k][0][1] for k in kept])
    other_q = lax.ppermute(mine_q, "tm", swap_cores)
    flag_q = (even | (partner == 0)).astype(jnp.int32)
    w_q = polar(jnp.stack([core, *ids(partner), flag_q]), mine_q, other_q, width, from_partner[FIRST:])
    at_end = jnp.stack([first | last]).astype(jnp.int32)
    begin, count, threshold = groups[e]
    cut = sum(a.shape[0] for a in from_partner[:FIRST])
    near, *far = turn(from_partner, w_q, [(0, 0, count), (1, 0, cut), (1, cut, count)])
    passes = [(p ^ 1, p - 1) for p in range(2, pairs, 2) if is_early(p, threshold)]
    passes += [(p ^ 1, p + 1) for p in range(1, pairs - 1, 2) if is_early(p, threshold)]
    passed = [(at, a.shape[0], lax.ppermute(a, "pair", passes)) for at, a in zip((0, cut), far)]
    alone = own(at_end, history, begin, count, w, far[:1])

    choice = jnp.stack([jnp.where(even, 1 + first, 0), jnp.where(even, 0, 1 + last)]).astype(jnp.int32)
    parts = [[(begin, count, (near, None, alone))], [], [], []]
    for at, size, a in passed:
        parts[1].append((begin + at, size, (None, a, None)))
    for k in kept:
        begin, count = groups[k][:2]
        for at, a, from_far in late_far[k]:
            parts[1].append((begin + at, a.shape[0], (None, from_far, a)))
        for part, (at, size, a) in zip(parts[2:], late_near[k]):
            part.append((begin + at, size, (a, None, None)))
    joined = join(choice, parts[0], rows, width)
    for part in parts[1:]:
        joined = join(choice, part, rows, width, joined, mark(joined), 56)
    return joined


def solution(mesh):
    in_specs = (P("tm", "pair"), P())
    out_specs = P("tm", "pair")
    return jax.shard_map(shards, mesh=mesh, in_specs=in_specs, out_specs=out_specs, check_vma=False)
```

```python
import jax
import jax.numpy as jnp
from jax import lax
from jax.experimental import pallas as pl
from jax.experimental.pallas import tpu as pltpu
from jax.sharding import PartitionSpec as P

STEPS = 4
TILE = 128
F32, BF16 = jnp.float32, jnp.bfloat16

epsilon = 1e-06

PLAN = ((0, (6, 11, 14)), (4, (33,)))
FIRST, LAST = 2, 6

MIB = 1 << 20
LONG = 10**12
WHOLE = pl.BlockSpec()
IN_VMEM = pl.BlockSpec(memory_space=pltpu.VMEM)
IN_SMEM = pl.BlockSpec(memory_space=pltpu.SMEM)
ANYWHERE = pl.BlockSpec(memory_space=pl.ANY)
IN_HBM = pl.BlockSpec(memory_space=pltpu.HBM)


def call(kernel, name, operands, in_specs, outs, out_specs, scratch=(), after=(), vmem=56, flops=0, after_spec=ANYWHERE, **more):
    given, late = len(operands), len(after)

    def body(*refs):
        kernel(*refs[:given], *refs[given + late :])

    return pl.pallas_call(
        body,
        in_specs=[*in_specs, *[after_spec] * late],
        out_specs=out_specs,
        out_shape=outs,
        scratch_shapes=scratch,
        compiler_params=pltpu.CompilerParams(vmem_limit_bytes=vmem * MIB),
        cost_estimate=pl.CostEstimate(flops=flops, bytes_accessed=0, transcendentals=0),
        name=name,
        **more,
    )(*operands, *after)


def shape(*dims, dtype=F32):
    return jax.ShapeDtypeStruct(dims, dtype)


def split(x):
    high = x.astype(BF16)
    return high, (x - high.astype(F32)).astype(BF16)


def product(a, b):
    return jnp.dot(a, b, preferred_element_type=F32)


def inner(a, b):
    return lax.dot_general(a, b, (((0,), (0,)), ((), ())), preferred_element_type=F32)


def packing(width):
    n = width // TILE
    above = [(i, j) for i in range(n) for j in range(i + 1, n)]
    shared = [(i, i + 1) for i in range(0, n, 2)]
    return [(above[h::2], shared[h::2]) for h in (0, 1)]


def packed_rows(width):
    above, shared = packing(width)[0]
    return (len(above) + len(shared)) * TILE + 16


def tile_at(i, j):
    return slice(i * TILE, (i + 1) * TILE), slice(j * TILE, (j + 1) * TILE)


def tile_indices():
    return (lax.broadcasted_iota(jnp.int32, (TILE, TILE), axis) for axis in (0, 1))


def gram(core, b, pieces, kept, after, parts=4):
    rows, width = b.shape

    def kernel(core_ref, b_ref, *refs):
        mine_ref, other_ref, *copies = refs[:-5]
        rows_ref, high_ref, cross_ref, load_sem, store_sem = refs[-5:]
        loads = [
            pltpu.make_async_copy(b_ref.at[pl.ds(p * (rows // parts), rows // parts)], at, load_sem.at[p])
            for p, at in enumerate(rows_ref.at[pl.ds(p * (rows // parts), rows // parts)] for p in range(parts))
        ]
        stores = [
            pltpu.make_async_copy(rows_ref.at[pl.ds(*piece)], copies[k], store_sem.at[k])
            for k, piece in enumerate((*pieces, *kept))
        ]
        for load in loads:
            load.start()
        for p, load in enumerate(loads):
            load.wait()
            high, low = split(rows_ref[p * (rows // parts) : (p + 1) * (rows // parts)])
            high_ref[p] = inner(high, high)
            cross_ref[p] = inner(high, low)
        for store in stores:
            store.start()

        def tile(i, j):
            there, mirrored = tile_at(i, j), tile_at(j, i)
            total = sum(high_ref[(p, *there)] + cross_ref[(p, *there)] for p in range(parts))
            return total + sum(cross_ref[(p, *mirrored)] for p in range(parts)).T

        row, column = tile_indices()
        for flag, outs in enumerate(((mine_ref, other_ref), (other_ref, mine_ref))):

            @pl.when(core_ref[0] == flag)
            def _():
                for out_ref, (above, shared) in zip(outs, packing(width)):
                    at = 0
                    for i, j in above:
                        out_ref[at : at + TILE, :] = tile(i, j)
                        at += TILE
                    diagonals = []
                    for i, j in shared:
                        one = tile(i, i)
                        out_ref[at : at + TILE, :] = jnp.where(row < column, one, tile(j, j))
                        diagonals.append(jnp.sum(jnp.where(row == column, one, 0.0), axis=0, keepdims=True))
                        at += TILE
                    out_ref[at:, :] = jnp.zeros_like(out_ref[at:, :])
                    for k, diagonal in enumerate(diagonals):
                        out_ref[at + k : at + k + 1, :] = diagonal

        for store in stores:
            store.wait()

    outs = [shape(packed_rows(width), TILE)] * 2 + [shape(count, width) for _, count in (*pieces, *kept)]
    scratch = [
        pltpu.VMEM((rows, width), F32),
        *[pltpu.VMEM((parts, width, width), F32)] * 2,
        pltpu.SemaphoreType.DMA((parts,)),
        pltpu.SemaphoreType.DMA((len(outs) - 2,)),
    ]
    specs = [IN_VMEM] * 2 + [ANYWHERE] * len(pieces) + [IN_VMEM] * len(kept)
    return call(kernel, "gram", (core, b), [IN_SMEM, ANYWHERE], outs, specs, scratch, after, 57, LONG)


def add(a, b, after):
    def kernel(a_ref, b_ref, out_ref):
        out_ref[...] = a_ref[...] + b_ref[...]

    return call(kernel, "add", (a, b), [IN_VMEM] * 2, shape(*a.shape), IN_VMEM, after=after, vmem=8)


def add_and_cut(second, a, b, after):
    n = a.shape[0] // 2

    def kernel(second_ref, a_ref, b_ref, out_ref, part_ref):
        out_ref[...] = a_ref[...] + b_ref[...]
        for flag, at in ((0, slice(0, n)), (1, slice(n, 2 * n))):

            @pl.when(second_ref[0] == flag)
            def _():
                part_ref[...] = a_ref[at, :] + b_ref[at, :]

    outs = [shape(*a.shape), shape(n, a.shape[1])]
    specs = [IN_SMEM, IN_VMEM, IN_VMEM]
    return call(kernel, "add", (second, a, b), specs, outs, [IN_VMEM] * 2, after=after, vmem=8)


def merge_kernel(second_ref, a_ref, b_ref, out_ref):
    n = a_ref.shape[0]
    for flag, (x_ref, y_ref) in enumerate(((a_ref, b_ref), (b_ref, a_ref))):

        @pl.when(second_ref[0] == flag)
        def _():
            out_ref[:n] = x_ref[...]
            out_ref[n:] = y_ref[...]


def merge(second, a, b, after):
    out = shape(2 * a.shape[0], a.shape[1])
    return call(merge_kernel, "merge", (second, a, b), [IN_SMEM, IN_VMEM, IN_VMEM], out, IN_VMEM, after=after, vmem=8)


def polar_kernel(at_ref, mine_ref, other_ref, high_ref, low_ref, x_ref, one_ref, two_ref):
    width = x_ref.shape[0]
    half = width // 2
    core, top_id, bottom_id, swapped = (at_ref[i] for i in range(4))
    tile_row, tile_column = tile_indices()
    for h, (above, shared) in enumerate(packing(width)):
        at = 0

        def taken(size):
            rows = slice(at, at + size)
            return jnp.where(core == h, mine_ref[rows, :], other_ref[rows, :])

        for i, j in above:
            tile = taken(TILE)
            one_ref[tile_at(i, j)] = tile
            one_ref[tile_at(j, i)] = tile.T
            at += TILE
        tiles = []
        for _ in shared:
            tiles.append(taken(TILE))
            at += TILE
        diagonals = taken(16)
        for k, ((i, j), tile) in enumerate(zip(shared, tiles)):
            mirrored = tile.T
            lower = jnp.where(tile_row > tile_column, mirrored, diagonals[k : k + 1, :])
            one_ref[tile_at(i, i)] = jnp.where(tile_row < tile_column, tile, lower)
            one_ref[tile_at(j, j)] = jnp.where(tile_row < tile_column, mirrored, tile)
    row = lax.broadcasted_iota(jnp.int32, (width, width), 0)
    column = lax.broadcasted_iota(jnp.int32, (width, width), 1)
    on_diagonal = row == column

    def global_id(c):
        return jnp.where(c < half, top_id * half + c, bottom_id * half + c - half)

    row_id = global_id(lax.broadcasted_iota(jnp.int32, (width, 1), 0))
    column_id = global_id(lax.broadcasted_iota(jnp.int32, (1, width), 1))
    gram_full = one_ref[...]
    diagonal = jnp.where(on_diagonal, gram_full, 0.0)
    across = jnp.sum(diagonal, axis=0, keepdims=True)
    down = jnp.sum(diagonal, axis=1, keepdims=True)
    skew = gram_full / (down + across + epsilon)
    skew = jnp.where(column_id > row_id, skew, jnp.where(column_id < row_id, -skew, 0.0))
    norm = jnp.sqrt(1.0 + jnp.sum(skew * skew))
    x_ref[...] = (jnp.where(on_diagonal, 1.0, 0.0) + skew) / norm
    for _ in range(STEPS):
        high, low = split(x_ref[...])
        one_ref[...] = inner(high, high)
        two_ref[...] = inner(high, low)
        square = one_ref[...] + two_ref[...] + two_ref[...].T
        turn_high, turn_low = split(jnp.where(on_diagonal, 1.5, 0.0) - 0.5 * square)
        x_ref[...] = product(high, turn_high)
        one_ref[...] = product(high, turn_low)
        two_ref[...] = product(low, turn_high)
        x_ref[...] = x_ref[...] + (one_ref[...] + two_ref[...])
    for flag, (first, second) in enumerate((((0, half), (half, width)), ((half, width), (0, half)))):

        @pl.when(swapped == flag)
        def _():
            for to, (begin, end) in ((0, first), (half, second)):
                high, low = split(x_ref[:, begin:end])
                high_ref[:, to : to + half] = high
                low_ref[:, to : to + half] = low


def polar(at, mine, other, width, after=()):
    specs = [IN_SMEM, IN_VMEM, IN_VMEM]
    outs = [shape(width, width, dtype=BF16)] * 2
    scratch = [pltpu.VMEM((width, width), F32)] * 3
    return call(polar_kernel, "polar", (at, mine, other), specs, outs, [IN_VMEM] * 2, scratch, after, 24, LONG, IN_HBM)


def times(rows, w_high, w_low):
    high, low = split(rows)
    return product(high, w_high) + product(high, w_low) + product(low, w_high)


def turn(arrays, w, wanted, after=(), spec=WHOLE):
    half = w[0].shape[0] // 2

    def kernel(*refs):
        (high_ref, low_ref), parts, outs = refs[:2], refs[2 : 2 + len(arrays)], refs[2 + len(arrays) :]
        for out_ref, (side, begin, end) in zip(outs, wanted):
            columns = slice(side * half, (side + 1) * half)
            w_high, w_low = high_ref[:, columns], low_ref[:, columns]
            at = 0
            for b_ref in parts:
                size = b_ref.shape[0]
                lower, upper = max(begin, at), min(end, at + size)
                if lower < upper:
                    out_ref[lower - begin : upper - begin, :] = times(b_ref[lower - at : upper - at, :], w_high, w_low)
                at += size

    outs = [shape(end - begin, half) for _, begin, end in wanted]
    specs = [WHOLE] * 2 + [spec] * len(arrays)
    return call(kernel, "turn", (*w, *arrays), specs, outs, [WHOLE] * len(outs), after=after, vmem=24)


def own(at_end, b, start, count, w, after=()):
    width = b.shape[1]
    half = width // 2

    def kernel(at_end_ref, b_ref, high_ref, low_ref, out_ref, rows_ref, sem):
        @pl.when(at_end_ref[0] == 1)
        def _():
            load = pltpu.make_async_copy(b_ref.at[pl.ds(start, count)], rows_ref, sem)
            load.start()
            load.wait()
            out_ref[...] = times(rows_ref[...], high_ref[:, half:], low_ref[:, half:])

    specs = [IN_SMEM, ANYWHERE, WHOLE, WHOLE]
    scratch = [pltpu.VMEM((count, width), F32), pltpu.SemaphoreType.DMA]
    return call(kernel, "own", (at_end, b, *w), specs, shape(count, half), IN_VMEM, scratch, after, 24)


def join(choice, groups, rows, width, into=None, token=None, vmem=8):
    places = []
    for start, count, sources in groups:
        for s, source in enumerate(sources):
            if source is not None:
                array, begin = source if isinstance(source, tuple) else (source, 0)
                places.append((start, count, s, array, begin))
    half = width // 2

    def kernel(choice_ref, *refs):
        out_ref, sem = refs[-2:]

        def each(act):
            for k, (start, count, s, _, begin) in enumerate(places):
                for side in (0, 1):
                    store = pltpu.make_async_copy(
                        refs[k].at[pl.ds(begin, count)],
                        out_ref.at[pl.ds(start, count), pl.ds(side * half, half)],
                        sem.at[k],
                    )

                    @pl.when(choice_ref[side] == s)
                    def _():
                        act(store)

        each(lambda store: store.start())
        each(lambda store: store.wait())

    operands = (choice, *[array for _, _, _, array, _ in places])
    specs = [IN_SMEM] + [IN_VMEM] * len(places)
    more = {}
    if into is not None:
        more["input_output_aliases"] = {len(operands): 0}
        operands += (into, token)
        specs += [ANYWHERE, ANYWHERE]
    scratch = [pltpu.SemaphoreType.DMA((len(places),))]
    return call(kernel, "join", operands, specs, shape(rows, width), ANYWHERE, scratch, vmem=vmem, **more)


def mark(after):
    def kernel(out_ref):
        out_ref[...] = jnp.zeros_like(out_ref)

    return call(kernel, "mark", (), [], shape(8, TILE), WHOLE, after=(after,))


def shards(history, round_index):
    rows, width = history.shape
    pairs = lax.axis_size("pair")
    levels = pairs // 2
    position = lax.axis_index("pair")
    partner = position ^ 1
    even = position % 2 == 0
    first, last = position == 0, position == pairs - 1
    core, row_half = lax.axis_index("tm") % 2, lax.axis_index("tm") // 2
    cycle_len = 2 * pairs - 1
    round_now = round_index[0]
    swap_pairs = [(p, p ^ 1) for p in range(pairs)]
    swap_cores = [(i, i ^ 1) for i in range(4)]
    swap_rows = [(i, i ^ 2) for i in range(4)]

    def ids(p):
        top_id = jnp.where(p == 0, 0, 1 + jnp.mod(p - 1 - round_now, cycle_len))
        bottom_id = 1 + jnp.mod(2 * pairs - 2 - p - round_now, cycle_len)
        return top_id, bottom_id

    def is_early(p, threshold):
        level = p // 2
        return (p % 2 == 0) & (level >= threshold) | (p % 2 == 1) & (level <= levels - 1 - threshold)

    groups, pieces = [], []
    begin = 0
    for quarter, parts in PLAN:
        counts = [rows * part // 64 for part in parts]
        groups.append((begin, sum(counts), quarter * levels // 4))
        pieces.append([(begin + sum(counts[:i]), count) for i, count in enumerate(counts)])
        begin += sum(counts)
    early = [k for k, group in enumerate(groups) if group[2] < levels]

    def sent_early(k, rows_of_k):
        return lax.ppermute(rows_of_k, "pair", [(p, p ^ 1) for p in range(pairs) if is_early(p, groups[k][2])])

    (e,) = early
    taken = [history[begin : begin + count] for begin, count in pieces[e][:FIRST]]
    from_partner = [sent_early(e, a) for a in taken]

    kept = [k for k in range(len(groups)) if groups[k][2] > 0]
    later = pieces[e][FIRST:]
    keep, give, *copies = gram(jnp.stack([core]), history, later, [groups[k][:2] for k in kept], taken)
    kept = dict(zip(kept, copies[len(later) :]))
    summed = add(keep, lax.ppermute(give, "tm", swap_cores), from_partner[:1])
    from_row = lax.ppermute(summed, "tm", swap_rows)
    second = jnp.stack([row_half])
    mine, part = add_and_cut(second, summed, from_row, ())
    other = lax.ppermute(mine, "tm", swap_cores)
    part = lax.ppermute(part, "pair", swap_pairs)
    from_partner += [sent_early(e, a) for a in copies[: len(later)]]

    flag = (~even | first).astype(jnp.int32)
    w = polar(jnp.stack([core, *ids(position), flag]), mine, other, width, (part, *from_partner[:FIRST]))
    to_partner, onward = {}, {}
    for k, (_, _, threshold) in enumerate(groups):
        to_partner[k] = [(p, p ^ 1) for p in range(pairs) if not is_early(p, threshold)]
        onward[k] = [(p, p - 1) for p in range(2, pairs, 2) if not is_early(p, threshold)]
        onward[k] += [(p, p + 1) for p in range(1, pairs - 1, 2) if not is_early(p, threshold)]
    late_near, late_far = {}, {}
    for k in kept:
        count = groups[k][1]
        cut = count - rows * LAST // 64
        two = turn([kept[k]], w, [(0, 0, cut), (0, cut, count)], spec=IN_VMEM)
        late_near[k] = [(at, a.shape[0], lax.ppermute(a, "pair", to_partner[k])) for at, a in zip((0, cut), two)]
        cut = count // 32 * 16
        two = turn([kept[k]], w, [(1, 0, cut), (1, cut, count)], two[:1], IN_VMEM)
        late_far[k] = [(at, a, lax.ppermute(a, "pair", onward[k])) for at, a in zip((0, cut), two)]

    part_2 = lax.ppermute(part, "tm", swap_rows)
    mine_q = merge(second, part, part_2, [late_far[k][0][1] for k in kept])
    other_q = lax.ppermute(mine_q, "tm", swap_cores)
    flag_q = (even | (partner == 0)).astype(jnp.int32)
    w_q = polar(jnp.stack([core, *ids(partner), flag_q]), mine_q, other_q, width, from_partner[FIRST:])
    at_end = jnp.stack([first | last]).astype(jnp.int32)
    begin, count, threshold = groups[e]
    cut = count * 3 // 5 // 32 * 32
    near, *far = turn(from_partner, w_q, [(0, 0, count), (1, 0, cut), (1, cut, count)])
    passes = [(p ^ 1, p - 1) for p in range(2, pairs, 2) if is_early(p, threshold)]
    passes += [(p ^ 1, p + 1) for p in range(1, pairs - 1, 2) if is_early(p, threshold)]
    passed = [(at, a.shape[0], lax.ppermute(a, "pair", passes)) for at, a in zip((0, cut), far)]
    alone = own(at_end, history, begin, count, w, far[:1])

    choice = jnp.stack([jnp.where(even, 1 + first, 0), jnp.where(even, 0, 1 + last)]).astype(jnp.int32)
    parts = [[(begin, count, (near, None, alone))], [], [], []]
    for at, size, a in passed:
        parts[1].append((begin + at, size, (None, a, None)))
    for k in kept:
        begin, count = groups[k][:2]
        for at, a, from_far in late_far[k]:
            parts[1].append((begin + at, a.shape[0], (None, from_far, a)))
        for part, (at, size, a) in zip(parts[2:], late_near[k]):
            part.append((begin + at, size, (a, None, None)))
    joined = join(choice, parts[0], rows, width)
    for part in parts[1:]:
        joined = join(choice, part, rows, width, joined, mark(joined), 56)
    return joined


def solution(mesh):
    in_specs = (P("tm", "pair"), P())
    out_specs = P("tm", "pair")
    return jax.shard_map(shards, mesh=mesh, in_specs=in_specs, out_specs=out_specs, check_vma=False)
```

```python
import jax
import jax.numpy as jnp
from jax import lax
from jax.experimental import pallas as pl
from jax.experimental.pallas import tpu as pltpu
from jax.sharding import PartitionSpec as P

STEPS = 4
TILE = 128
F32, BF16 = jnp.float32, jnp.bfloat16

epsilon = 1e-06

PLAN = ((0, (6, 10, 15)), (4, (33,)))
FIRST, LAST = 2, 6

MIB = 1 << 20
LONG = 10**12
WHOLE = pl.BlockSpec()
IN_VMEM = pl.BlockSpec(memory_space=pltpu.VMEM)
IN_SMEM = pl.BlockSpec(memory_space=pltpu.SMEM)
ANYWHERE = pl.BlockSpec(memory_space=pl.ANY)
IN_HBM = pl.BlockSpec(memory_space=pltpu.HBM)


def call(kernel, name, operands, in_specs, outs, out_specs, scratch=(), after=(), vmem=56, flops=0, after_spec=ANYWHERE, **more):
    given, late = len(operands), len(after)

    def body(*refs):
        kernel(*refs[:given], *refs[given + late :])

    return pl.pallas_call(
        body,
        in_specs=[*in_specs, *[after_spec] * late],
        out_specs=out_specs,
        out_shape=outs,
        scratch_shapes=scratch,
        compiler_params=pltpu.CompilerParams(vmem_limit_bytes=vmem * MIB),
        cost_estimate=pl.CostEstimate(flops=flops, bytes_accessed=0, transcendentals=0),
        name=name,
        **more,
    )(*operands, *after)


def shape(*dims, dtype=F32):
    return jax.ShapeDtypeStruct(dims, dtype)


def split(x):
    high = x.astype(BF16)
    return high, (x - high.astype(F32)).astype(BF16)


def product(a, b):
    return jnp.dot(a, b, preferred_element_type=F32)


def inner(a, b):
    return lax.dot_general(a, b, (((0,), (0,)), ((), ())), preferred_element_type=F32)


def packing(width):
    n = width // TILE
    above = [(i, j) for i in range(n) for j in range(i + 1, n)]
    shared = [(i, i + 1) for i in range(0, n, 2)]
    return [(above[h::2], shared[h::2]) for h in (0, 1)]


def packed_rows(width):
    above, shared = packing(width)[0]
    return (len(above) + len(shared)) * TILE + 16


def tile_at(i, j):
    return slice(i * TILE, (i + 1) * TILE), slice(j * TILE, (j + 1) * TILE)


def tile_indices():
    return (lax.broadcasted_iota(jnp.int32, (TILE, TILE), axis) for axis in (0, 1))


def gram(core, b, pieces, kept, after, parts=4):
    rows, width = b.shape

    def kernel(core_ref, b_ref, *refs):
        mine_ref, other_ref, *copies = refs[:-5]
        rows_ref, high_ref, cross_ref, load_sem, store_sem = refs[-5:]
        loads = [
            pltpu.make_async_copy(b_ref.at[pl.ds(p * (rows // parts), rows // parts)], at, load_sem.at[p])
            for p, at in enumerate(rows_ref.at[pl.ds(p * (rows // parts), rows // parts)] for p in range(parts))
        ]
        stores = [
            pltpu.make_async_copy(rows_ref.at[pl.ds(*piece)], copies[k], store_sem.at[k])
            for k, piece in enumerate((*pieces, *kept))
        ]
        for load in loads:
            load.start()
        for p, load in enumerate(loads):
            load.wait()
            high, low = split(rows_ref[p * (rows // parts) : (p + 1) * (rows // parts)])
            high_ref[p] = inner(high, high)
            cross_ref[p] = inner(high, low)
        for store in stores:
            store.start()

        def tile(i, j):
            there, mirrored = tile_at(i, j), tile_at(j, i)
            total = sum(high_ref[(p, *there)] + cross_ref[(p, *there)] for p in range(parts))
            return total + sum(cross_ref[(p, *mirrored)] for p in range(parts)).T

        row, column = tile_indices()
        for flag, outs in enumerate(((mine_ref, other_ref), (other_ref, mine_ref))):

            @pl.when(core_ref[0] == flag)
            def _():
                for out_ref, (above, shared) in zip(outs, packing(width)):
                    at = 0
                    for i, j in above:
                        out_ref[at : at + TILE, :] = tile(i, j)
                        at += TILE
                    diagonals = []
                    for i, j in shared:
                        one = tile(i, i)
                        out_ref[at : at + TILE, :] = jnp.where(row < column, one, tile(j, j))
                        diagonals.append(jnp.sum(jnp.where(row == column, one, 0.0), axis=0, keepdims=True))
                        at += TILE
                    out_ref[at:, :] = jnp.zeros_like(out_ref[at:, :])
                    for k, diagonal in enumerate(diagonals):
                        out_ref[at + k : at + k + 1, :] = diagonal

        for store in stores:
            store.wait()

    outs = [shape(packed_rows(width), TILE)] * 2 + [shape(count, width) for _, count in (*pieces, *kept)]
    scratch = [
        pltpu.VMEM((rows, width), F32),
        *[pltpu.VMEM((parts, width, width), F32)] * 2,
        pltpu.SemaphoreType.DMA((parts,)),
        pltpu.SemaphoreType.DMA((len(outs) - 2,)),
    ]
    specs = [IN_VMEM] * 2 + [ANYWHERE] * len(pieces) + [IN_VMEM] * len(kept)
    return call(kernel, "gram", (core, b), [IN_SMEM, IN_HBM], outs, specs, scratch, after, 32, LONG)


def add(a, b, after):
    def kernel(a_ref, b_ref, out_ref):
        out_ref[...] = a_ref[...] + b_ref[...]

    return call(kernel, "add", (a, b), [IN_VMEM] * 2, shape(*a.shape), IN_VMEM, after=after, vmem=8)


def add_and_cut(second, a, b, after):
    n = a.shape[0] // 2

    def kernel(second_ref, a_ref, b_ref, out_ref, part_ref):
        out_ref[...] = a_ref[...] + b_ref[...]
        for flag, at in ((0, slice(0, n)), (1, slice(n, 2 * n))):

            @pl.when(second_ref[0] == flag)
            def _():
                part_ref[...] = a_ref[at, :] + b_ref[at, :]

    outs = [shape(*a.shape), shape(n, a.shape[1])]
    specs = [IN_SMEM, IN_VMEM, IN_VMEM]
    return call(kernel, "add", (second, a, b), specs, outs, [IN_VMEM] * 2, after=after, vmem=8)


def merge_kernel(second_ref, a_ref, b_ref, out_ref):
    n = a_ref.shape[0]
    for flag, (x_ref, y_ref) in enumerate(((a_ref, b_ref), (b_ref, a_ref))):

        @pl.when(second_ref[0] == flag)
        def _():
            out_ref[:n] = x_ref[...]
            out_ref[n:] = y_ref[...]


def merge(second, a, b, after):
    out = shape(2 * a.shape[0], a.shape[1])
    return call(merge_kernel, "merge", (second, a, b), [IN_SMEM, IN_VMEM, IN_VMEM], out, IN_VMEM, after=after, vmem=8)


def polar_kernel(at_ref, mine_ref, other_ref, high_ref, low_ref, x_ref, one_ref, two_ref):
    width = x_ref.shape[0]
    half = width // 2
    core, top_id, bottom_id, swapped = (at_ref[i] for i in range(4))
    tile_row, tile_column = tile_indices()
    for h, (above, shared) in enumerate(packing(width)):
        at = 0

        def taken(size):
            rows = slice(at, at + size)
            return jnp.where(core == h, mine_ref[rows, :], other_ref[rows, :])

        for i, j in above:
            tile = taken(TILE)
            one_ref[tile_at(i, j)] = tile
            one_ref[tile_at(j, i)] = tile.T
            at += TILE
        tiles = []
        for _ in shared:
            tiles.append(taken(TILE))
            at += TILE
        diagonals = taken(16)
        for k, ((i, j), tile) in enumerate(zip(shared, tiles)):
            mirrored = tile.T
            lower = jnp.where(tile_row > tile_column, mirrored, diagonals[k : k + 1, :])
            one_ref[tile_at(i, i)] = jnp.where(tile_row < tile_column, tile, lower)
            one_ref[tile_at(j, j)] = jnp.where(tile_row < tile_column, mirrored, tile)
    row = lax.broadcasted_iota(jnp.int32, (width, width), 0)
    column = lax.broadcasted_iota(jnp.int32, (width, width), 1)
    on_diagonal = row == column

    def global_id(c):
        return jnp.where(c < half, top_id * half + c, bottom_id * half + c - half)

    row_id = global_id(lax.broadcasted_iota(jnp.int32, (width, 1), 0))
    column_id = global_id(lax.broadcasted_iota(jnp.int32, (1, width), 1))
    gram_full = one_ref[...]
    diagonal = jnp.where(on_diagonal, gram_full, 0.0)
    across = jnp.sum(diagonal, axis=0, keepdims=True)
    down = jnp.sum(diagonal, axis=1, keepdims=True)
    skew = gram_full / (down + across + epsilon)
    skew = jnp.where(column_id > row_id, skew, jnp.where(column_id < row_id, -skew, 0.0))
    norm = jnp.sqrt(1.0 + jnp.sum(skew * skew))
    x_ref[...] = (jnp.where(on_diagonal, 1.0, 0.0) + skew) / norm
    for _ in range(STEPS):
        high, low = split(x_ref[...])
        one_ref[...] = inner(high, high)
        two_ref[...] = inner(high, low)
        square = one_ref[...] + two_ref[...] + two_ref[...].T
        turn_high, turn_low = split(jnp.where(on_diagonal, 1.5, 0.0) - 0.5 * square)
        x_ref[...] = product(high, turn_high)
        one_ref[...] = product(high, turn_low)
        two_ref[...] = product(low, turn_high)
        x_ref[...] = x_ref[...] + (one_ref[...] + two_ref[...])
    for flag, (first, second) in enumerate((((0, half), (half, width)), ((half, width), (0, half)))):

        @pl.when(swapped == flag)
        def _():
            for to, (begin, end) in ((0, first), (half, second)):
                high, low = split(x_ref[:, begin:end])
                high_ref[:, to : to + half] = high
                low_ref[:, to : to + half] = low


def polar(at, mine, other, width, after=()):
    specs = [IN_SMEM, IN_VMEM, IN_VMEM]
    outs = [shape(width, width, dtype=BF16)] * 2
    scratch = [pltpu.VMEM((width, width), F32)] * 3
    return call(polar_kernel, "polar", (at, mine, other), specs, outs, [IN_VMEM] * 2, scratch, after, 24, LONG, IN_HBM)


def times(rows, w_high, w_low):
    high, low = split(rows)
    return product(high, w_high) + product(high, w_low) + product(low, w_high)


def turn(arrays, w, wanted, after=(), spec=WHOLE):
    half = w[0].shape[0] // 2

    def kernel(*refs):
        (high_ref, low_ref), parts, outs = refs[:2], refs[2 : 2 + len(arrays)], refs[2 + len(arrays) :]
        for out_ref, (side, begin, end) in zip(outs, wanted):
            columns = slice(side * half, (side + 1) * half)
            w_high, w_low = high_ref[:, columns], low_ref[:, columns]
            at = 0
            for b_ref in parts:
                size = b_ref.shape[0]
                lower, upper = max(begin, at), min(end, at + size)
                if lower < upper:
                    out_ref[lower - begin : upper - begin, :] = times(b_ref[lower - at : upper - at, :], w_high, w_low)
                at += size

    outs = [shape(end - begin, half) for _, begin, end in wanted]
    specs = [WHOLE] * 2 + [spec] * len(arrays)
    return call(kernel, "turn", (*w, *arrays), specs, outs, [WHOLE] * len(outs), after=after, vmem=24)


def own(at_end, b, start, count, w, after=()):
    width = b.shape[1]
    half = width // 2

    def kernel(at_end_ref, b_ref, high_ref, low_ref, out_ref, rows_ref, sem):
        @pl.when(at_end_ref[0] == 1)
        def _():
            load = pltpu.make_async_copy(b_ref.at[pl.ds(start, count)], rows_ref, sem)
            load.start()
            load.wait()
            out_ref[...] = times(rows_ref[...], high_ref[:, half:], low_ref[:, half:])

    specs = [IN_SMEM, IN_HBM, WHOLE, WHOLE]
    scratch = [pltpu.VMEM((count, width), F32), pltpu.SemaphoreType.DMA]
    return call(kernel, "own", (at_end, b, *w), specs, shape(count, half), IN_VMEM, scratch, after, 24)


def join(choice, groups, rows, width, into=None, token=None, vmem=8):
    places = []
    for start, count, sources in groups:
        for s, source in enumerate(sources):
            if source is not None:
                array, begin = source if isinstance(source, tuple) else (source, 0)
                places.append((start, count, s, array, begin))
    half = width // 2

    def kernel(choice_ref, *refs):
        out_ref, sem = refs[-2:]

        def each(act):
            for k, (start, count, s, _, begin) in enumerate(places):
                for side in (0, 1):
                    store = pltpu.make_async_copy(
                        refs[k].at[pl.ds(begin, count)],
                        out_ref.at[pl.ds(start, count), pl.ds(side * half, half)],
                        sem.at[k],
                    )

                    @pl.when(choice_ref[side] == s)
                    def _():
                        act(store)

        each(lambda store: store.start())
        each(lambda store: store.wait())

    operands = (choice, *[array for _, _, _, array, _ in places])
    specs = [IN_SMEM] + [IN_VMEM] * len(places)
    more = {}
    if into is not None:
        more["input_output_aliases"] = {len(operands): 0}
        operands += (into, token)
        specs += [ANYWHERE, ANYWHERE]
    scratch = [pltpu.SemaphoreType.DMA((len(places),))]
    return call(kernel, "join", operands, specs, shape(rows, width), ANYWHERE, scratch, vmem=vmem, **more)


def mark(after):
    def kernel(out_ref):
        out_ref[...] = jnp.zeros_like(out_ref)

    return call(kernel, "mark", (), [], shape(8, TILE), WHOLE, after=(after,))


def shards(history, round_index):
    rows, width = history.shape
    pairs = lax.axis_size("pair")
    levels = pairs // 2
    position = lax.axis_index("pair")
    partner = position ^ 1
    even = position % 2 == 0
    first, last = position == 0, position == pairs - 1
    core, row_half = lax.axis_index("tm") % 2, lax.axis_index("tm") // 2
    cycle_len = 2 * pairs - 1
    round_now = round_index[0]
    swap_pairs = [(p, p ^ 1) for p in range(pairs)]
    swap_cores = [(i, i ^ 1) for i in range(4)]
    swap_rows = [(i, i ^ 2) for i in range(4)]

    def ids(p):
        top_id = jnp.where(p == 0, 0, 1 + jnp.mod(p - 1 - round_now, cycle_len))
        bottom_id = 1 + jnp.mod(2 * pairs - 2 - p - round_now, cycle_len)
        return top_id, bottom_id

    def is_early(p, threshold):
        level = p // 2
        return (p % 2 == 0) & (level >= threshold) | (p % 2 == 1) & (level <= levels - 1 - threshold)

    groups, pieces = [], []
    begin = 0
    for quarter, parts in PLAN:
        counts = [rows * part // 64 for part in parts]
        groups.append((begin, sum(counts), quarter * levels // 4))
        pieces.append([(begin + sum(counts[:i]), count) for i, count in enumerate(counts)])
        begin += sum(counts)
    early = [k for k, group in enumerate(groups) if group[2] < levels]

    def sent_early(k, rows_of_k):
        return lax.ppermute(rows_of_k, "pair", [(p, p ^ 1) for p in range(pairs) if is_early(p, groups[k][2])])

    (e,) = early
    taken = [history[begin : begin + count] for begin, count in pieces[e][:FIRST]]
    from_partner = [sent_early(e, a) for a in taken]

    kept = [k for k in range(len(groups)) if groups[k][2] > 0]
    later = pieces[e][FIRST:]
    keep, give, *copies = gram(jnp.stack([core]), history, later, [groups[k][:2] for k in kept], taken)
    kept = dict(zip(kept, copies[len(later) :]))
    summed = add(keep, lax.ppermute(give, "tm", swap_cores), from_partner[:1])
    from_row = lax.ppermute(summed, "tm", swap_rows)
    second = jnp.stack([row_half])
    mine, part = add_and_cut(second, summed, from_row, ())
    other = lax.ppermute(mine, "tm", swap_cores)
    part = lax.ppermute(part, "pair", swap_pairs)
    from_partner += [sent_early(e, a) for a in copies[: len(later)]]

    flag = (~even | first).astype(jnp.int32)
    w = polar(jnp.stack([core, *ids(position), flag]), mine, other, width, (part, *from_partner[:FIRST]))
    to_partner, onward = {}, {}
    for k, (_, _, threshold) in enumerate(groups):
        to_partner[k] = [(p, p ^ 1) for p in range(pairs) if not is_early(p, threshold)]
        onward[k] = [(p, p - 1) for p in range(2, pairs, 2) if not is_early(p, threshold)]
        onward[k] += [(p, p + 1) for p in range(1, pairs - 1, 2) if not is_early(p, threshold)]
    late_near, late_far = {}, {}
    for k in kept:
        count = groups[k][1]
        cut = count - rows * LAST // 64
        two = turn([kept[k]], w, [(0, 0, cut), (0, cut, count)], spec=IN_VMEM)
        late_near[k] = [(at, a.shape[0], lax.ppermute(a, "pair", to_partner[k])) for at, a in zip((0, cut), two)]
        cut = count // 32 * 16
        two = turn([kept[k]], w, [(1, 0, cut), (1, cut, count)], two[:1], IN_VMEM)
        late_far[k] = [(at, a, lax.ppermute(a, "pair", onward[k])) for at, a in zip((0, cut), two)]

    part_2 = lax.ppermute(part, "tm", swap_rows)
    mine_q = merge(second, part, part_2, [late_far[k][0][1] for k in kept])
    other_q = lax.ppermute(mine_q, "tm", swap_cores)
    flag_q = (even | (partner == 0)).astype(jnp.int32)
    w_q = polar(jnp.stack([core, *ids(partner), flag_q]), mine_q, other_q, width, from_partner[FIRST:])
    at_end = jnp.stack([first | last]).astype(jnp.int32)
    begin, count, threshold = groups[e]
    cut = count * 3 // 5 // 32 * 32
    near, *far = turn(from_partner, w_q, [(0, 0, count), (1, 0, cut), (1, cut, count)])
    passes = [(p ^ 1, p - 1) for p in range(2, pairs, 2) if is_early(p, threshold)]
    passes += [(p ^ 1, p + 1) for p in range(1, pairs - 1, 2) if is_early(p, threshold)]
    passed = [(at, a.shape[0], lax.ppermute(a, "pair", passes)) for at, a in zip((0, cut), far)]
    alone = own(at_end, history, begin, count, w, far[:1])

    choice = jnp.stack([jnp.where(even, 1 + first, 0), jnp.where(even, 0, 1 + last)]).astype(jnp.int32)
    parts = [[(begin, count, (near, None, alone))], [], [], []]
    for at, size, a in passed:
        parts[1].append((begin + at, size, (None, a, None)))
    for k in kept:
        begin, count = groups[k][:2]
        for at, a, from_far in late_far[k]:
            parts[1].append((begin + at, a.shape[0], (None, from_far, a)))
        for part, (at, size, a) in zip(parts[2:], late_near[k]):
            part.append((begin + at, size, (a, None, None)))
    joined = join(choice, parts[0], rows, width)
    for part in parts[1:]:
        joined = join(choice, part, rows, width, joined, mark(joined), 56)
    return joined


def solution(mesh):
    in_specs = (P("tm", "pair"), P())
    out_specs = P("tm", "pair")
    return jax.shard_map(shards, mesh=mesh, in_specs=in_specs, out_specs=out_specs, check_vma=False)
```

```python
import jax
import jax.numpy as jnp
from jax import lax
from jax.experimental import pallas as pl
from jax.experimental.pallas import tpu as pltpu
from jax.sharding import PartitionSpec as P

STEPS = 4
TILE = 128
F32, BF16 = jnp.float32, jnp.bfloat16

epsilon = 1e-06

PLAN = ((0, (6, 10, 14)), (4, (34,)))
FIRST, LAST = 2, 6

MIB = 1 << 20
LONG = 10**12
WHOLE = pl.BlockSpec()
IN_VMEM = pl.BlockSpec(memory_space=pltpu.VMEM)
IN_SMEM = pl.BlockSpec(memory_space=pltpu.SMEM)
ANYWHERE = pl.BlockSpec(memory_space=pl.ANY)
IN_HBM = pl.BlockSpec(memory_space=pltpu.HBM)


def call(kernel, name, operands, in_specs, outs, out_specs, scratch=(), after=(), vmem=56, flops=0, after_spec=ANYWHERE, **more):
    given, late = len(operands), len(after)

    def body(*refs):
        kernel(*refs[:given], *refs[given + late :])

    return pl.pallas_call(
        body,
        in_specs=[*in_specs, *[after_spec] * late],
        out_specs=out_specs,
        out_shape=outs,
        scratch_shapes=scratch,
        compiler_params=pltpu.CompilerParams(vmem_limit_bytes=vmem * MIB),
        cost_estimate=pl.CostEstimate(flops=flops, bytes_accessed=0, transcendentals=0),
        name=name,
        **more,
    )(*operands, *after)


def shape(*dims, dtype=F32):
    return jax.ShapeDtypeStruct(dims, dtype)


def split(x):
    high = x.astype(BF16)
    return high, (x - high.astype(F32)).astype(BF16)


def product(a, b):
    return jnp.dot(a, b, preferred_element_type=F32)


def inner(a, b):
    return lax.dot_general(a, b, (((0,), (0,)), ((), ())), preferred_element_type=F32)


def packing(width):
    n = width // TILE
    above = [(i, j) for i in range(n) for j in range(i + 1, n)]
    shared = [(i, i + 1) for i in range(0, n, 2)]
    return [(above[h::2], shared[h::2]) for h in (0, 1)]


def packed_rows(width):
    above, shared = packing(width)[0]
    return (len(above) + len(shared)) * TILE + 16


def tile_at(i, j):
    return slice(i * TILE, (i + 1) * TILE), slice(j * TILE, (j + 1) * TILE)


def tile_indices():
    return (lax.broadcasted_iota(jnp.int32, (TILE, TILE), axis) for axis in (0, 1))


def gram(core, b, pieces, kept, after, parts=4):
    rows, width = b.shape

    def kernel(core_ref, b_ref, *refs):
        mine_ref, other_ref, *copies = refs[:-5]
        rows_ref, high_ref, cross_ref, load_sem, store_sem = refs[-5:]
        loads = [
            pltpu.make_async_copy(b_ref.at[pl.ds(p * (rows // parts), rows // parts)], at, load_sem.at[p])
            for p, at in enumerate(rows_ref.at[pl.ds(p * (rows // parts), rows // parts)] for p in range(parts))
        ]
        stores = [
            pltpu.make_async_copy(rows_ref.at[pl.ds(*piece)], copies[k], store_sem.at[k])
            for k, piece in enumerate((*pieces, *kept))
        ]
        for load in loads:
            load.start()
        for p, load in enumerate(loads):
            load.wait()
            high, low = split(rows_ref[p * (rows // parts) : (p + 1) * (rows // parts)])
            high_ref[p] = inner(high, high)
            cross_ref[p] = inner(high, low)
        for store in stores:
            store.start()

        def tile(i, j):
            there, mirrored = tile_at(i, j), tile_at(j, i)
            total = sum(high_ref[(p, *there)] + cross_ref[(p, *there)] for p in range(parts))
            return total + sum(cross_ref[(p, *mirrored)] for p in range(parts)).T

        row, column = tile_indices()
        for flag, outs in enumerate(((mine_ref, other_ref), (other_ref, mine_ref))):

            @pl.when(core_ref[0] == flag)
            def _():
                for out_ref, (above, shared) in zip(outs, packing(width)):
                    at = 0
                    for i, j in above:
                        out_ref[at : at + TILE, :] = tile(i, j)
                        at += TILE
                    diagonals = []
                    for i, j in shared:
                        one = tile(i, i)
                        out_ref[at : at + TILE, :] = jnp.where(row < column, one, tile(j, j))
                        diagonals.append(jnp.sum(jnp.where(row == column, one, 0.0), axis=0, keepdims=True))
                        at += TILE
                    out_ref[at:, :] = jnp.zeros_like(out_ref[at:, :])
                    for k, diagonal in enumerate(diagonals):
                        out_ref[at + k : at + k + 1, :] = diagonal

        for store in stores:
            store.wait()

    outs = [shape(packed_rows(width), TILE)] * 2 + [shape(count, width) for _, count in (*pieces, *kept)]
    scratch = [
        pltpu.VMEM((rows, width), F32),
        *[pltpu.VMEM((parts, width, width), F32)] * 2,
        pltpu.SemaphoreType.DMA((parts,)),
        pltpu.SemaphoreType.DMA((len(outs) - 2,)),
    ]
    specs = [IN_VMEM] * 2 + [ANYWHERE] * len(pieces) + [IN_VMEM] * len(kept)
    return call(kernel, "gram", (core, b), [IN_SMEM, IN_HBM], outs, specs, scratch, after, 32, LONG)


def add(a, b, after):
    def kernel(a_ref, b_ref, out_ref):
        out_ref[...] = a_ref[...] + b_ref[...]

    return call(kernel, "add", (a, b), [IN_VMEM] * 2, shape(*a.shape), IN_VMEM, after=after, vmem=8)


def add_and_cut(second, a, b, after):
    n = a.shape[0] // 2

    def kernel(second_ref, a_ref, b_ref, out_ref, part_ref):
        out_ref[...] = a_ref[...] + b_ref[...]
        for flag, at in ((0, slice(0, n)), (1, slice(n, 2 * n))):

            @pl.when(second_ref[0] == flag)
            def _():
                part_ref[...] = a_ref[at, :] + b_ref[at, :]

    outs = [shape(*a.shape), shape(n, a.shape[1])]
    specs = [IN_SMEM, IN_VMEM, IN_VMEM]
    return call(kernel, "add", (second, a, b), specs, outs, [IN_VMEM] * 2, after=after, vmem=8)


def merge_kernel(second_ref, a_ref, b_ref, out_ref):
    n = a_ref.shape[0]
    for flag, (x_ref, y_ref) in enumerate(((a_ref, b_ref), (b_ref, a_ref))):

        @pl.when(second_ref[0] == flag)
        def _():
            out_ref[:n] = x_ref[...]
            out_ref[n:] = y_ref[...]


def merge(second, a, b, after):
    out = shape(2 * a.shape[0], a.shape[1])
    return call(merge_kernel, "merge", (second, a, b), [IN_SMEM, IN_VMEM, IN_VMEM], out, IN_VMEM, after=after, vmem=8)


def polar_kernel(at_ref, mine_ref, other_ref, high_ref, low_ref, x_ref, one_ref, two_ref):
    width = x_ref.shape[0]
    half = width // 2
    core, top_id, bottom_id, swapped = (at_ref[i] for i in range(4))
    tile_row, tile_column = tile_indices()
    for h, (above, shared) in enumerate(packing(width)):
        at = 0

        def taken(size):
            rows = slice(at, at + size)
            return jnp.where(core == h, mine_ref[rows, :], other_ref[rows, :])

        for i, j in above:
            tile = taken(TILE)
            one_ref[tile_at(i, j)] = tile
            one_ref[tile_at(j, i)] = tile.T
            at += TILE
        tiles = []
        for _ in shared:
            tiles.append(taken(TILE))
            at += TILE
        diagonals = taken(16)
        for k, ((i, j), tile) in enumerate(zip(shared, tiles)):
            mirrored = tile.T
            lower = jnp.where(tile_row > tile_column, mirrored, diagonals[k : k + 1, :])
            one_ref[tile_at(i, i)] = jnp.where(tile_row < tile_column, tile, lower)
            one_ref[tile_at(j, j)] = jnp.where(tile_row < tile_column, mirrored, tile)
    row = lax.broadcasted_iota(jnp.int32, (width, width), 0)
    column = lax.broadcasted_iota(jnp.int32, (width, width), 1)
    on_diagonal = row == column

    def global_id(c):
        return jnp.where(c < half, top_id * half + c, bottom_id * half + c - half)

    row_id = global_id(lax.broadcasted_iota(jnp.int32, (width, 1), 0))
    column_id = global_id(lax.broadcasted_iota(jnp.int32, (1, width), 1))
    gram_full = one_ref[...]
    diagonal = jnp.where(on_diagonal, gram_full, 0.0)
    across = jnp.sum(diagonal, axis=0, keepdims=True)
    down = jnp.sum(diagonal, axis=1, keepdims=True)
    skew = gram_full / (down + across + epsilon)
    skew = jnp.where(column_id > row_id, skew, jnp.where(column_id < row_id, -skew, 0.0))
    norm = jnp.sqrt(1.0 + jnp.sum(skew * skew))
    x_ref[...] = (jnp.where(on_diagonal, 1.0, 0.0) + skew) / norm
    for _ in range(STEPS):
        high, low = split(x_ref[...])
        one_ref[...] = inner(high, high)
        two_ref[...] = inner(high, low)
        square = one_ref[...] + two_ref[...] + two_ref[...].T
        turn_high, turn_low = split(jnp.where(on_diagonal, 1.5, 0.0) - 0.5 * square)
        x_ref[...] = product(high, turn_high)
        one_ref[...] = product(high, turn_low)
        two_ref[...] = product(low, turn_high)
        x_ref[...] = x_ref[...] + (one_ref[...] + two_ref[...])
    for flag, (first, second) in enumerate((((0, half), (half, width)), ((half, width), (0, half)))):

        @pl.when(swapped == flag)
        def _():
            for to, (begin, end) in ((0, first), (half, second)):
                high, low = split(x_ref[:, begin:end])
                high_ref[:, to : to + half] = high
                low_ref[:, to : to + half] = low


def polar(at, mine, other, width, after=()):
    specs = [IN_SMEM, IN_VMEM, IN_VMEM]
    outs = [shape(width, width, dtype=BF16)] * 2
    scratch = [pltpu.VMEM((width, width), F32)] * 3
    return call(polar_kernel, "polar", (at, mine, other), specs, outs, [IN_VMEM] * 2, scratch, after, 24, LONG, IN_HBM)


def times(rows, w_high, w_low):
    high, low = split(rows)
    return product(high, w_high) + product(high, w_low) + product(low, w_high)


def turn(arrays, w, wanted, after=(), spec=WHOLE):
    half = w[0].shape[0] // 2

    def kernel(*refs):
        (high_ref, low_ref), parts, outs = refs[:2], refs[2 : 2 + len(arrays)], refs[2 + len(arrays) :]
        for out_ref, (side, begin, end) in zip(outs, wanted):
            columns = slice(side * half, (side + 1) * half)
            w_high, w_low = high_ref[:, columns], low_ref[:, columns]
            at = 0
            for b_ref in parts:
                size = b_ref.shape[0]
                lower, upper = max(begin, at), min(end, at + size)
                if lower < upper:
                    out_ref[lower - begin : upper - begin, :] = times(b_ref[lower - at : upper - at, :], w_high, w_low)
                at += size

    outs = [shape(end - begin, half) for _, begin, end in wanted]
    specs = [WHOLE] * 2 + [spec] * len(arrays)
    return call(kernel, "turn", (*w, *arrays), specs, outs, [WHOLE] * len(outs), after=after, vmem=24)


def own(at_end, b, start, count, w, after=()):
    width = b.shape[1]
    half = width // 2

    def kernel(at_end_ref, b_ref, high_ref, low_ref, out_ref, rows_ref, sem):
        @pl.when(at_end_ref[0] == 1)
        def _():
            load = pltpu.make_async_copy(b_ref.at[pl.ds(start, count)], rows_ref, sem)
            load.start()
            load.wait()
            out_ref[...] = times(rows_ref[...], high_ref[:, half:], low_ref[:, half:])

    specs = [IN_SMEM, IN_HBM, WHOLE, WHOLE]
    scratch = [pltpu.VMEM((count, width), F32), pltpu.SemaphoreType.DMA]
    return call(kernel, "own", (at_end, b, *w), specs, shape(count, half), IN_VMEM, scratch, after, 24)


def join(choice, groups, rows, width, into=None, token=None, vmem=8):
    places = []
    for start, count, sources in groups:
        for s, source in enumerate(sources):
            if source is not None:
                array, begin = source if isinstance(source, tuple) else (source, 0)
                places.append((start, count, s, array, begin))
    half = width // 2

    def kernel(choice_ref, *refs):
        out_ref, sem = refs[-2:]

        def each(act):
            for k, (start, count, s, _, begin) in enumerate(places):
                for side in (0, 1):
                    store = pltpu.make_async_copy(
                        refs[k].at[pl.ds(begin, count)],
                        out_ref.at[pl.ds(start, count), pl.ds(side * half, half)],
                        sem.at[k],
                    )

                    @pl.when(choice_ref[side] == s)
                    def _():
                        act(store)

        each(lambda store: store.start())
        each(lambda store: store.wait())

    operands = (choice, *[array for _, _, _, array, _ in places])
    specs = [IN_SMEM] + [IN_VMEM] * len(places)
    more = {}
    if into is not None:
        more["input_output_aliases"] = {len(operands): 0}
        operands += (into, token)
        specs += [ANYWHERE, ANYWHERE]
    scratch = [pltpu.SemaphoreType.DMA((len(places),))]
    return call(kernel, "join", operands, specs, shape(rows, width), ANYWHERE, scratch, vmem=vmem, **more)


def mark(after):
    def kernel(out_ref):
        out_ref[...] = jnp.zeros_like(out_ref)

    return call(kernel, "mark", (), [], shape(8, TILE), WHOLE, after=(after,))


def shards(history, round_index):
    rows, width = history.shape
    pairs = lax.axis_size("pair")
    levels = pairs // 2
    position = lax.axis_index("pair")
    partner = position ^ 1
    even = position % 2 == 0
    first, last = position == 0, position == pairs - 1
    core, row_half = lax.axis_index("tm") % 2, lax.axis_index("tm") // 2
    cycle_len = 2 * pairs - 1
    round_now = round_index[0]
    swap_pairs = [(p, p ^ 1) for p in range(pairs)]
    swap_cores = [(i, i ^ 1) for i in range(4)]
    swap_rows = [(i, i ^ 2) for i in range(4)]

    def ids(p):
        top_id = jnp.where(p == 0, 0, 1 + jnp.mod(p - 1 - round_now, cycle_len))
        bottom_id = 1 + jnp.mod(2 * pairs - 2 - p - round_now, cycle_len)
        return top_id, bottom_id

    def is_early(p, threshold):
        level = p // 2
        return (p % 2 == 0) & (level >= threshold) | (p % 2 == 1) & (level <= levels - 1 - threshold)

    groups, pieces = [], []
    begin = 0
    for quarter, parts in PLAN:
        counts = [rows * part // 64 for part in parts]
        groups.append((begin, sum(counts), quarter * levels // 4))
        pieces.append([(begin + sum(counts[:i]), count) for i, count in enumerate(counts)])
        begin += sum(counts)
    early = [k for k, group in enumerate(groups) if group[2] < levels]

    def sent_early(k, rows_of_k):
        return lax.ppermute(rows_of_k, "pair", [(p, p ^ 1) for p in range(pairs) if is_early(p, groups[k][2])])

    (e,) = early
    taken = [history[begin : begin + count] for begin, count in pieces[e][:FIRST]]
    from_partner = [sent_early(e, a) for a in taken]

    kept = [k for k in range(len(groups)) if groups[k][2] > 0]
    later = pieces[e][FIRST:]
    keep, give, *copies = gram(jnp.stack([core]), history, later, [groups[k][:2] for k in kept], taken)
    kept = dict(zip(kept, copies[len(later) :]))
    summed = add(keep, lax.ppermute(give, "tm", swap_cores), from_partner[:1])
    from_row = lax.ppermute(summed, "tm", swap_rows)
    second = jnp.stack([row_half])
    mine, part = add_and_cut(second, summed, from_row, ())
    other = lax.ppermute(mine, "tm", swap_cores)
    part = lax.ppermute(part, "pair", swap_pairs)
    from_partner += [sent_early(e, a) for a in copies[: len(later)]]

    flag = (~even | first).astype(jnp.int32)
    w = polar(jnp.stack([core, *ids(position), flag]), mine, other, width, (part, *from_partner[:FIRST]))
    to_partner, onward = {}, {}
    for k, (_, _, threshold) in enumerate(groups):
        to_partner[k] = [(p, p ^ 1) for p in range(pairs) if not is_early(p, threshold)]
        onward[k] = [(p, p - 1) for p in range(2, pairs, 2) if not is_early(p, threshold)]
        onward[k] += [(p, p + 1) for p in range(1, pairs - 1, 2) if not is_early(p, threshold)]
    late_near, late_far = {}, {}
    for k in kept:
        count = groups[k][1]
        cut = count - rows * LAST // 64
        two = turn([kept[k]], w, [(0, 0, cut), (0, cut, count)], spec=IN_VMEM)
        late_near[k] = [(at, a.shape[0], lax.ppermute(a, "pair", to_partner[k])) for at, a in zip((0, cut), two)]
        cut = count // 32 * 16
        two = turn([kept[k]], w, [(1, 0, cut), (1, cut, count)], two[:1], IN_VMEM)
        late_far[k] = [(at, a, lax.ppermute(a, "pair", onward[k])) for at, a in zip((0, cut), two)]

    part_2 = lax.ppermute(part, "tm", swap_rows)
    mine_q = merge(second, part, part_2, [late_far[k][0][1] for k in kept])
    other_q = lax.ppermute(mine_q, "tm", swap_cores)
    flag_q = (even | (partner == 0)).astype(jnp.int32)
    w_q = polar(jnp.stack([core, *ids(partner), flag_q]), mine_q, other_q, width, from_partner[FIRST:])
    at_end = jnp.stack([first | last]).astype(jnp.int32)
    begin, count, threshold = groups[e]
    cut = count * 3 // 5 // 32 * 32
    near, *far = turn(from_partner, w_q, [(0, 0, count), (1, 0, cut), (1, cut, count)])
    passes = [(p ^ 1, p - 1) for p in range(2, pairs, 2) if is_early(p, threshold)]
    passes += [(p ^ 1, p + 1) for p in range(1, pairs - 1, 2) if is_early(p, threshold)]
    passed = [(at, a.shape[0], lax.ppermute(a, "pair", passes)) for at, a in zip((0, cut), far)]
    alone = own(at_end, history, begin, count, w, far[:1])

    choice = jnp.stack([jnp.where(even, 1 + first, 0), jnp.where(even, 0, 1 + last)]).astype(jnp.int32)
    parts = [[(begin, count, (near, None, alone))], [], [], []]
    for at, size, a in passed:
        parts[1].append((begin + at, size, (None, a, None)))
    for k in kept:
        begin, count = groups[k][:2]
        for at, a, from_far in late_far[k]:
            parts[1].append((begin + at, a.shape[0], (None, from_far, a)))
        for part, (at, size, a) in zip(parts[2:], late_near[k]):
            part.append((begin + at, size, (a, None, None)))
    joined = join(choice, parts[0], rows, width)
    for part in parts[1:]:
        joined = join(choice, part, rows, width, joined, mark(joined), 56)
    return joined


def solution(mesh):
    in_specs = (P("tm", "pair"), P())
    out_specs = P("tm", "pair")
    return jax.shard_map(shards, mesh=mesh, in_specs=in_specs, out_specs=out_specs, check_vma=False)
```
